512 devices in a mesh: level: 4 (over z_lo), tx: 8 (over x, core), ty: 16 (over y, z_hi).
Axes of the slice: x: 4, y: 4, z: 16 (z_hi: 4, z_lo: 4; z = z_hi * 4 + z_lo), core: 2. Of those that a mesh axis runs over, the one named last changes fastest.
Arguments:
- initial: float32 [48, 256, 2048], P(None, 'tx', 'ty'), may hold values from -6 to 6
- layer_ids: int32 [48], replicated, may hold values from 0 to 5
- lateral_number: float32 [6], replicated, may hold values from 0.05 to 0.24
- vertical_number: float32 [6], replicated, may hold values from 0.5 to 8
- pulse_rates: float32 [8], replicated, may hold values from 0.5 to 4
- bore_x: int32 [1024], replicated, may hold values from 0 to 255
- bore_y: int32 [1024], replicated, may hold values from 0 to 2047
- plan: int32 [1024, 7], replicated, may hold values from 0 to 7
Outputs:
- states: float32 [4, 48, 256, 2048], P('level', None, 'tx', 'ty')
The draws below stay inside these ranges and needn't reach their ends.
All inputs are finite; a program needn't handle non-finite values.
Results may differ from the reference program's by a relative error of at most 0.00022.
Values sent between devices are 32-bit elements; how exact they have to be, the bound alone decides.
No kernel may reach another device: no remote copies, remote signals or barrier semaphores. Data moves between devices by JAX's collectives and lax.ppermute only.
A program may use at most 128 MiB of HBM per device.

```python
import math
import jax
import jax.numpy as jnp
from jax import lax

NZ = 48
STEPS = 6
NLAYER = 6
NPULSE = 8
LEVELS = 4
NX = 256
NY = 2048
BORES = 1024


def set_ends(drawn, rng, smallest, high):
    extent = drawn.shape
    index_at = [jax.random.randint(jax.random.fold_in(rng, axis), (), 0, extent[axis]) for axis in range(len(extent))]
    drawn = drawn.at[tuple(index_at)].set(smallest)
    longest = extent.index(max(extent))
    index_at[longest] = (index_at[longest] + 1) % extent[longest]
    return drawn.at[tuple(index_at)].set(high)


def level_of(rng, extent, shards, smallest, largest):
    factor_of = 1.0
    for dim, parts in shards:
        steps = jax.random.uniform(jax.random.fold_in(jax.random.fold_in(rng, 6), dim), (parts,), jnp.float32, smallest / len(shards), largest / len(shards))
        factor_of = factor_of * jnp.repeat(jnp.exp(steps), extent[dim] // parts).reshape((-1,) + (1,) * (len(extent) - 1 - dim))
    return factor_of


def bell_draw(key, extent, scale, bound, shards=(), held_as=jnp.bfloat16):
    result = scale * jax.random.normal(key, extent, jnp.float32)
    if shards:
        result = result * level_of(key, extent, shards, -0.22, 0.18)
    return jnp.clip(result, -bound, bound).astype(held_as)


def setup_inputs(seed: int = 0) -> dict:
    arg_keys = jax.random.split(jax.random.key(seed), 9)
    initial = bell_draw(arg_keys[0], (NZ, NX, NY), 1.0, 6.0, ((1, 8), (2, 16)), jnp.float32)
    layer_ids = set_ends(jax.random.randint(arg_keys[1], (NZ,), 0, NLAYER), jax.random.fold_in(arg_keys[1], 1), 0, NLAYER - 1).astype(jnp.int32)
    lateral_number = jnp.clip(jnp.exp(jax.random.uniform(arg_keys[2], (NLAYER,), jnp.float32, math.log(0.05), math.log(0.24))), 0.05, 0.24)
    vertical_number = jnp.clip(jnp.exp(jax.random.uniform(arg_keys[3], (NLAYER,), jnp.float32, math.log(0.5), math.log(8.0))), 0.5, 8.0)
    pulse_rates = jnp.clip(jnp.exp(jax.random.uniform(arg_keys[4], (NPULSE,), jnp.float32, math.log(0.5), math.log(4.0))), 0.5, 4.0)
    bore_x = set_ends(jax.random.randint(arg_keys[5], (BORES,), 0, NX), jax.random.fold_in(arg_keys[5], 1), 0, NX - 1).astype(jnp.int32)
    bore_y = set_ends(jax.random.randint(arg_keys[6], (BORES,), 0, NY), jax.random.fold_in(arg_keys[6], 1), 0, NY - 1).astype(jnp.int32)
    plan = set_ends(jax.random.randint(arg_keys[7], (BORES, STEPS + 1), 0, NPULSE), jax.random.fold_in(arg_keys[7], 1), 0, NPULSE - 1).astype(jnp.int32)
    return dict(initial=initial, layer_ids=layer_ids, lateral_number=lateral_number, vertical_number=vertical_number, pulse_rates=pulse_rates, bore_x=bore_x, bore_y=bore_y, plan=plan)


def vertical(layer_ids, lateral_number, vertical_number):
    kinds = jnp.arange(NLAYER, dtype=jnp.int32)
    onehot = (layer_ids[:, None] == kinds[None, :]).astype(jnp.float32)
    cond = jnp.sum(onehot * vertical_number[None, :], axis=1)
    lat_depth = jnp.sum(onehot * lateral_number[None, :], axis=1)
    link = 2.0 * cond[:-1] * cond[1:] / (cond[:-1] + cond[1:])
    zero_one = jnp.zeros((1,), jnp.float32)
    diagonal = jnp.concatenate([cond[:1], jnp.zeros((NZ - 1,), jnp.float32)])
    diagonal = diagonal + jnp.concatenate([link, zero_one]) + jnp.concatenate([zero_one, link])
    vertical_op = jnp.diag(diagonal) - jnp.diag(link, 1) - jnp.diag(link, -1)
    eye = jnp.eye(NZ, dtype=jnp.float32)
    lower_band = jnp.concatenate([zero_one, -link])
    upper_band = jnp.concatenate([-link, zero_one])
    inverse_block = lax.linalg.tridiagonal_solve(lower_band, 1.0 + diagonal, upper_band, eye)
    return (vertical_op, inverse_block, lat_depth)

def along_depth(matrix, field):
    return jnp.einsum('ij,jxy->ixy', matrix, field, precision=lax.Precision.HIGHEST)

def depth_profile():
    depth = jnp.arange(NZ, dtype=jnp.int32)
    return ((depth >= 2) & (depth < NZ - 4)).astype(jnp.float32)

def lateral_term(field, lat_depth):
    padded = jnp.pad(field, ((0, 0), (1, 1), (1, 1)))
    center = padded[:, 1:-1, 1:-1]
    beside = padded[:, 2:, 1:-1] + padded[:, :-2, 1:-1] + padded[:, 1:-1, 2:] + padded[:, 1:-1, :-2]
    return lat_depth[:, None, None] * (beside - 4.0 * center)

def source_at(point, pulse_rates, bore_x, bore_y, plan):
    levels = jnp.arange(NPULSE, dtype=jnp.int32)
    picked = (plan[:, point][:, None] == levels[None, :]).astype(jnp.float32)
    rate_bore = jnp.sum(picked * pulse_rates[None, :], axis=1)
    plane = jnp.zeros((NX, NY), jnp.float32).at[bore_x, bore_y].add(rate_bore)
    return depth_profile()[:, None, None] * plane[None, :, :]

def reference(initial, layer_ids, lateral_number, vertical_number, pulse_rates, bore_x, bore_y, plan):
    vertical_op, inverse_block, lat_depth = vertical(layer_ids, lateral_number, vertical_number)
    sources = [source_at(point, pulse_rates, bore_x, bore_y, plan) for point in range(STEPS + 1)]
    state = initial
    low_states = [state]
    low_lateral = [lateral_term(state, lat_depth)]
    for step in range(STEPS):
        state = along_depth(inverse_block, state + low_lateral[step] + sources[step])
        low_states.append(state)
        low_lateral.append(lateral_term(state, lat_depth))
    finals = [state]
    for level_id in range(1, LEVELS):
        flux = [low_lateral[k] - along_depth(vertical_op, low_states[k]) + sources[k] for k in range(STEPS + 1)]
        state = initial
        own_lateral = lateral_term(state, lat_depth)
        new_states = [state]
        new_lateral = [own_lateral]
        for step in range(STEPS):
            if step == 0:
                quad = 0.5 * flux[0] + 0.5 * flux[1]
            else:
                quad = -flux[step - 1] / 12.0 + 8.0 * flux[step] / 12.0 + 5.0 * flux[step + 1] / 12.0
            rhs = state + own_lateral - low_lateral[step] + along_depth(vertical_op, low_states[step + 1]) + quad
            state = along_depth(inverse_block, rhs)
            own_lateral = lateral_term(state, lat_depth)
            new_states.append(state)
            new_lateral.append(own_lateral)
        finals.append(state)
        low_states = new_states
        low_lateral = new_lateral
    return jnp.stack(finals)
```

```python
import functools

import jax
import jax.numpy as jnp
from jax import lax
from jax.experimental import pallas as pl
from jax.experimental.pallas import tpu as pltpu
from jax.sharding import PartitionSpec as P

NZ = 48
STEPS = 6
NLAYER = 6
NPULSE = 8
LEVELS = 4
POWERS = STEPS + LEVELS
HALO = POWERS - 1
ROWS = 32
LANES = 128
EXT = ROWS + 2 * HALO
ZS = NZ + 8
PER_TILE = LANES // HALO
TILES = -(-EXT // PER_TILE)
DEPTH = 1152
VMEM = 48 * 1024 * 1024
F32, BF16 = jnp.float32, jnp.bfloat16


def split(x):
    high = x.astype(BF16)
    return high, (x - high.astype(F32)).astype(BF16)


def edge_rows(u_ref, top_ref, bottom_ref):
    for i in range(HALO):
        top_ref[i] = u_ref[pl.ds(i, NZ, stride=ROWS), :]
        bottom_ref[i] = u_ref[pl.ds(ROWS - HALO + i, NZ, stride=ROWS), :]


def ext_row(r, u_ref, above_ref, below_ref):
    if r < HALO:
        return above_ref[r]
    if r < HALO + ROWS:
        return u_ref[pl.ds(r - HALO, NZ, stride=ROWS), :]
    return below_ref[r - HALO - ROWS]


def edge_columns(place_ref, u_ref, above_ref, below_ref, packed_ref):
    lane = lax.broadcasted_iota(jnp.int32, (NZ, LANES), 1)
    from_right = jnp.where(place_ref[0] >= 2, HALO, 0)
    for t in range(TILES):
        tile = jnp.zeros((NZ, LANES), F32)
        for s in range(min(PER_TILE, EXT - t * PER_TILE)):
            row = ext_row(t * PER_TILE + s, u_ref, above_ref, below_ref)
            row = pltpu.roll(row, HALO * s + from_right, axis=1)
            tile = jnp.where((lane >= HALO * s) & (lane < HALO * (s + 1)), row, tile)
        packed_ref[t] = tile


def sources(place_ref, rates_ref, plan_ref, x_ref, y_ref, centre_ref, side_ref):
    bores = plan_ref.shape[1]
    plan = plan_ref[...]
    rate = jnp.zeros(plan.shape, F32)
    for j in range(NPULSE):
        rate = jnp.where(plan == j, rates_ref[j], rate)
    rate_high = rate.astype(BF16).astype(F32)
    rate_low = rate - rate_high
    cell_x = place_ref[1] * ROWS - HALO + lax.broadcasted_iota(jnp.int32, (ZS, bores), 0)
    hit_x = x_ref[...] == cell_x
    cell_y = lax.broadcasted_iota(jnp.int32, (2 * LANES, bores), 0)
    cell_y = jnp.where(cell_y >= LANES + LANES // 2, cell_y - 2 * LANES, cell_y)
    hit_y = (y_ref[...] == cell_y + place_ref[2] * LANES).astype(F32).astype(BF16)

    def plane(rates):
        left = [jnp.where(hit_x, rates[m : m + 1], 0.0) for m in range(STEPS + 1)]
        left = jnp.concatenate(left, axis=0).astype(BF16)
        return lax.dot_general(left, hit_y, (((1,), (1,)), ((), ())), preferred_element_type=F32)

    both = plane(rate_high) + plane(rate_low)
    for m in range(STEPS + 1):
        rows = both[m * ZS : (m + 1) * ZS]
        centre_ref[pl.ds(m, ZS, stride=8), :] = rows[:, :LANES]
        side_ref[pl.ds(m, ZS, stride=8), :] = rows[:, LANES:]
    blank = jnp.zeros((ZS, LANES), F32)
    centre_ref[pl.ds(7, ZS, stride=8), :] = blank
    side_ref[pl.ds(7, ZS, stride=8), :] = blank


def coefs(place_ref, lateral_ref, vertical_ref, ids_ref, out_ref, poly_ref, final_ref):
    ids = jnp.broadcast_to(ids_ref[...], (8, LANES))
    lane = lax.broadcasted_iota(jnp.int32, (8, LANES), 1)
    cond, lat = jnp.zeros((8, LANES), F32), jnp.zeros((8, LANES), F32)
    for j in range(NLAYER):
        cond = jnp.where(ids == j, vertical_ref[j], cond)
        lat = jnp.where(ids == j, lateral_ref[j], lat)
    cond = jnp.where(lane < NZ, cond, 1.0)
    lat = jnp.where(lane < NZ, lat, 0.0)
    after = pltpu.roll(cond, LANES - 1, axis=1)
    link = jnp.where(lane < NZ - 1, 2.0 * cond * after / (cond + after), 0.0)
    before = pltpu.roll(link, 1, axis=1)
    low, up = -before, -link
    mid = 1.0 + (jnp.where(lane == 0, cond, 0.0) + link + before)
    mid = jnp.where(lane < NZ, mid, 1.0)
    row_id = lax.broadcasted_iota(jnp.int32, (NZ, LANES), 0)
    lane_id = lax.broadcasted_iota(jnp.int32, (NZ, LANES), 1)
    rhs = (row_id == lane_id).astype(F32)
    wide = lambda v: jnp.broadcast_to(v[:1], (NZ, LANES))
    for s in (1, 2, 4, 8, 16, 32):
        back = lambda v: pltpu.roll(v, s, axis=1)
        forth = lambda v: pltpu.roll(v, LANES - s, axis=1)
        alpha = -low / back(mid)
        gamma = -up / forth(mid)
        rhs = rhs + wide(alpha) * back(rhs) + wide(gamma) * forth(rhs)
        mid = mid + alpha * back(up) + gamma * forth(low)
        low, up = alpha * back(low), gamma * forth(up)
    inverse = rhs / wide(mid)
    inverse = jnp.concatenate([inverse, jnp.zeros((LANES - NZ, LANES), F32)], axis=0)
    high = inverse.astype(BF16).astype(F32)
    weights = high + pltpu.roll(inverse - high, 64, axis=1)
    weights = jnp.concatenate([weights, high], axis=0).astype(BF16)

    def solve(blocks):
        high, low = split(jnp.concatenate(blocks, axis=0))
        both = jnp.dot(jnp.concatenate([high, low], axis=1), weights, preferred_element_type=F32)
        return both + pltpu.roll(both, 64, axis=1)

    row_id = lax.broadcasted_iota(jnp.int32, (ZS, LANES), 0)
    lane_id = lax.broadcasted_iota(jnp.int32, (ZS, LANES), 1)
    eye = ((row_id == lane_id) & (row_id < NZ)).astype(F32)
    profile = (lane_id >= 2) & (lane_id < NZ - 4)
    source = [((row_id == NZ + n) & profile).astype(F32) for n in range(STEPS + 1)]
    slope = jnp.broadcast_to(lat[:1], (ZS, LANES))
    stay = 1.0 - 4.0 * slope

    degree = lambda p, n: 0 if n == 0 else n + p

    def get(p, n, k):
        if k > degree(p, n):
            return None
        return eye if n == 0 else poly_ref[p, n, k * ZS : (k + 1) * ZS, :]

    def total(*terms):
        terms = [(f, t) for f, t in terms if t is not None]
        result = None
        for f, t in terms:
            t = t if f in (1.0, -1.0) else f * t
            if result is None:
                result = -t if f == -1.0 else t
            else:
                result = result - t if f == -1.0 else result + t
        return result

    def step(p, n):
        count = degree(p, n + 1) + 1
        blocks, rest, last = [], [], None
        for k in range(count):
            if p == 0:
                g = get(0, n, k)
                tail, add = None, source[n]
            else:
                b, c = get(p - 1, n, k), get(p - 1, n + 1, k)
                if n == 0:
                    w = total((0.5, b), (0.5, c))
                    g, add = w, 0.5 * source[0] + 0.5 * source[1]
                else:
                    w = total((-1.0 / 12.0, get(p - 1, n - 1, k)), (8.0 / 12.0, b), (5.0 / 12.0, c))
                    g = total((1.0, get(p, n, k)), (-1.0, b), (1.0, w))
                    add = (-source[n - 1] + 8.0 * source[n] + 5.0 * source[n + 1]) * (1.0 / 12.0)
                tail = total((1.0, b), (-1.0, c))
                rest.append(total((1.0, c), (-1.0, w)))
            parts = [
                (1.0, None if g is None else stay * g),
                (1.0, None if last is None else slope * last),
                (1.0, tail),
                (1.0, add if k == 0 else None),
            ]
            blocks.append(total(*parts))
            last = g
        solved = solve(blocks)
        for k in range(count):
            block = solved[k * ZS : (k + 1) * ZS]
            if p > 0 and rest[k] is not None:
                block = block + rest[k]
            poly_ref[p, n + 1, k * ZS : (k + 1) * ZS, :] = block

    for p in range(LEVELS):
        first = (degree(p, STEPS) + 1) * ZS
        if first < POWERS * ZS:
            poly_ref[p, STEPS, first:, :] = jnp.zeros((POWERS * ZS - first, LANES), F32)
    for wave in range(STEPS + LEVELS - 1):
        for p in range(LEVELS):
            if 0 <= wave - p < STEPS:
                step(p, wave - p)

    level = place_ref[0]
    for k in range(POWERS):
        block = poly_ref[level, STEPS, k * ZS : (k + 1) * ZS, :]
        final_ref[2 * k * ZS : (2 * k + 1) * ZS, :] = block
        final_ref[(2 * k + 1) * ZS : (2 * k + 2) * ZS, :] = block
    final_ref[2 * POWERS * ZS :, :] = jnp.zeros((DEPTH - 2 * POWERS * ZS, LANES), F32)
    table = final_ref[...].T[:NZ]
    high = table.astype(BF16).astype(F32)
    out_ref[...] = jnp.concatenate([high, table - high], axis=0).astype(BF16)


def evolve(
    place_ref, u_ref, above_ref, below_ref, own_ref, other_ref, src_centre_ref, src_side_ref, coef_ref,
    out_ref, centre_ref, side_ref, terms_ref,
):
    level, tx, ty = place_ref[0], place_ref[1], place_ref[2]
    lane = lax.broadcasted_iota(jnp.int32, (ZS, LANES), 1)
    lane_z = lax.broadcasted_iota(jnp.int32, (NZ, LANES), 1)
    low_level = level < 2
    for t in range(TILES):
        own, other = own_ref[t], other_ref[t]
        left = jnp.where(low_level, own, other)
        right = jnp.where(low_level, other, own)
        for s in range(min(PER_TILE, EXT - t * PER_TILE)):
            r = t * PER_TILE + s
            from_right = pltpu.roll(right, (LANES - HALO * s) % LANES, axis=1)
            from_left = pltpu.roll(left, (LANES - HALO * s - HALO) % LANES, axis=1)
            side_ref[0, r, :NZ, :] = jnp.where(lane_z < LANES // 2, from_right, from_left)
            centre_ref[0, r, :NZ, :] = ext_row(r, u_ref, above_ref, below_ref)
            centre_ref[0, r, NZ:, :] = src_centre_ref[8 * r : 8 * r + 8, :]
            side_ref[0, r, NZ:, :] = src_side_ref[8 * r : 8 * r + 8, :]

    def keep_terms(k, pair, half, c):
        high = c.astype(BF16).astype(F32)
        both = jnp.concatenate([high, c - high], axis=0).astype(BF16)
        terms_ref[pair, 2 * k * ZS : 2 * (k + 1) * ZS, half * LANES : (half + 1) * LANES] = both

    @pl.loop(0, ROWS // 2)
    def _(pair):
        terms_ref[pair, 2 * POWERS * ZS :, :] = jnp.zeros((DEPTH - 2 * POWERS * ZS, 2 * LANES), BF16)
        for half in range(2):
            keep_terms(0, pair, half, centre_ref[0, HALO + 2 * pair + half])

    last_x, last_y = place_ref[3], place_ref[4]
    inside = ((lane >= LANES // 2) | (ty < last_y)) & ((lane < LANES // 2) | (ty > 0))
    inside = inside.astype(F32)
    above_in = jnp.where(tx > 0, 1.0, 0.0)
    below_in = jnp.where(tx < last_x, 1.0, 0.0)
    first_lane, last_lane = lane == 0, lane == LANES - 1

    def neighbours(source, r):
        c, h = centre_ref[source, r], side_ref[source, r]
        c1, h1 = pltpu.roll(c, 1, axis=1), pltpu.roll(h, 1, axis=1)
        c2, h2 = pltpu.roll(c, LANES - 1, axis=1), pltpu.roll(h, LANES - 1, axis=1)
        new_c = centre_ref[source, r - 1] + centre_ref[source, r + 1]
        new_c += jnp.where(first_lane, h1, c1) + jnp.where(last_lane, h2, c2)
        new_h = side_ref[source, r - 1] + side_ref[source, r + 1]
        new_h += jnp.where(first_lane, c1, h1) + jnp.where(last_lane, c2, h2)
        return new_c, new_h * inside

    for k in range(1, POWERS):
        source, target = (k - 1) % 2, k % 2

        @pl.loop(0, ROWS // 2)
        def _(pair):
            for half in range(2):
                r = HALO + 2 * pair + half
                new_c, new_h = neighbours(source, r)
                centre_ref[target, r] = new_c
                side_ref[target, r] = new_h
                keep_terms(k, pair, half, new_c)

        if k < HALO:

            @pl.loop(k, HALO)
            def _(r):
                for row, there in ((r, above_in), (EXT - 1 - r, below_in)):
                    new_c, new_h = neighbours(source, row)
                    centre_ref[target, row] = new_c * there
                    side_ref[target, row] = new_h * there

    table = coef_ref[...]

    @pl.loop(0, ROWS // 2)
    def _(pair):
        both = jnp.dot(table, terms_ref[pair], preferred_element_type=F32)
        both = both[:NZ] + both[NZ:]
        out_ref[pl.ds(2 * pair, NZ, stride=ROWS), :] = both[:, :LANES]
        out_ref[pl.ds(2 * pair + 1, NZ, stride=ROWS), :] = both[:, LANES:]


SMEM = pl.BlockSpec(memory_space=pltpu.SMEM)
WHOLE = pl.BlockSpec(memory_space=pltpu.VMEM)


def call(kernel, name, ins, outs, scratch=(), cost=0):
    return pl.pallas_call(
        kernel,
        out_shape=outs,
        in_specs=ins,
        out_specs=jax.tree.map(lambda _: WHOLE, outs),
        scratch_shapes=list(scratch),
        compiler_params=pltpu.CompilerParams(vmem_limit_bytes=VMEM),
        cost_estimate=pl.CostEstimate(flops=cost, bytes_accessed=1 << 20, transcendentals=0),
        name=name,
    )


def on_device(initial, layer_ids, lateral_number, vertical_number, pulse_rates, bore_x, bore_y, plan):
    shape = lambda *s, dtype=F32: jax.ShapeDtypeStruct(s, dtype)
    count_x, count_y = lax.axis_size("tx"), lax.axis_size("ty")
    indices = [lax.axis_index(name) for name in ("level", "tx", "ty")]
    place = jnp.stack(indices + [jnp.int32(count_x - 1), jnp.int32(count_y - 1)])
    flat = initial.reshape(NZ * ROWS, LANES)
    slab = shape(HALO, NZ, LANES)
    top, bottom = call(edge_rows, "edge_rows", [WHOLE], (slab, slab))(flat)
    up = [(i, i + 1) for i in range(count_x - 1)]
    above = lax.ppermute(bottom, "tx", up)
    below = lax.ppermute(top, "tx", [(j, i) for i, j in up])
    strips = call(edge_columns, "edge_columns", [SMEM] + [WHOLE] * 3, shape(TILES, NZ, LANES))(
        place, flat, above, below
    )
    route = []
    for i in range(count_y - 1):
        for l in (0, 1):
            route.append(((l + 2) * count_y + i, l * count_y + i + 1))
            route.append((l * count_y + i + 1, (l + 2) * count_y + i))
    own = lax.ppermute(strips, ("level", "ty"), route)
    other = lax.ppermute(own, "level", [(0, 2), (2, 0), (1, 3), (3, 1)])

    planes = shape(ZS * 8, LANES)
    src_centre, src_side = call(sources, "sources", [SMEM] * 2 + [WHOLE] * 3, (planes, planes), cost=1 << 28)(
        place, pulse_rates, plan.T, bore_x[None, :], bore_y[None, :]
    )
    ids = jnp.pad(layer_ids, (0, LANES - NZ))[None, :]
    table = call(
        coefs,
        "coefs",
        [SMEM] * 3 + [WHOLE],
        shape(2 * NZ, DEPTH, dtype=BF16),
        [pltpu.VMEM((LEVELS, STEPS + 1, POWERS * ZS, LANES), F32), pltpu.VMEM((DEPTH, LANES), F32)],
        cost=1 << 28,
    )(place, lateral_number, vertical_number, ids)
    buffer = pltpu.VMEM((2, EXT, ZS, LANES), F32)
    result = call(
        evolve,
        "evolve",
        [SMEM] + [WHOLE] * 8,
        shape(NZ * ROWS, LANES),
        [buffer, buffer, pltpu.VMEM((ROWS // 2, DEPTH, 2 * LANES), BF16)],
    )(place, flat, above, below, own, other, src_centre, src_side, table)
    return result.reshape(1, NZ, ROWS, LANES)


def solution(mesh):
    return jax.shard_map(
        on_device,
        mesh=mesh,
        in_specs=(P(None, "tx", "ty"), P(), P(), P(), P(), P(), P(), P()),
        out_specs=P("level", None, "tx", "ty"),
        check_vma=False,
    )
```

```python
import jax
import jax.numpy as jnp
import numpy as np
from jax import lax
from jax.experimental import pallas as pl
from jax.experimental.pallas import tpu as pltpu
from jax.sharding import PartitionSpec as P

NZ = 48
STEPS = 6
NLAYER = 6
NPULSE = 8
LEVELS = 4
POWERS = STEPS + LEVELS
HALO = POWERS - 1
ROWS = 32
LANES = 128
EXT = ROWS + 2 * HALO
ZS = NZ + 8
HALF = ROWS // 2
PAIRS = HALF + 2 * HALO
SLOT = LANES // 2
BLOCKS = 8
SPAN = -(-(LANES + 2 * HALO) // BLOCKS)
WIDE = SPAN * BLOCKS
CHUNK = 5
VMEM = 48 * 1024 * 1024
F32, BF16 = jnp.float32, jnp.bfloat16


def pieces():
    width = [HALO - max(HALO - r, r - (HALO + ROWS - 1), 0) for r in range(EXT)]
    slots = [[r] for r in range(EXT) if width[r] == HALO]
    for d in range(1, (HALO + 1) // 2):
        slots.append([HALO - d, d])
        slots.append([EXT - 1 - (HALO - d), EXT - 1 - d])
    where, per_tile = {}, LANES // HALO
    for n, rows in enumerate(slots):
        lane = HALO * (n % per_tile)
        for r in rows:
            where[r] = (n // per_tile, lane, width[r])
            lane += width[r]
    return where, -(-len(slots) // per_tile)


PIECES, TILES = pieces()


def split(x):
    high = x.astype(BF16)
    return high, (x - high.astype(F32)).astype(BF16)


def edge_rows(u_ref, top_ref, bottom_ref):
    for i in range(HALO):
        top_ref[i] = u_ref[pl.ds(i, NZ, stride=ROWS), :]
        bottom_ref[i] = u_ref[pl.ds(ROWS - HALO + i, NZ, stride=ROWS), :]


def ext_row(r, u_ref, above_ref, below_ref):
    if r < HALO:
        return above_ref[r]
    if r < HALO + ROWS:
        return u_ref[pl.ds(r - HALO, NZ, stride=ROWS), :]
    return below_ref[r - HALO - ROWS]


def edge_columns(place_ref, u_ref, above_ref, below_ref, packed_ref):
    lane = lax.broadcasted_iota(jnp.int32, (NZ, LANES), 1)
    send_last = place_ref[0] >= 2
    tiles = [jnp.zeros((NZ, LANES), F32) for _ in range(TILES)]
    for r, (t, first, width) in PIECES.items():
        row = ext_row(r, u_ref, above_ref, below_ref)
        row = pltpu.roll(row, first + jnp.where(send_last, width, 0), axis=1)
        tiles[t] = jnp.where((lane >= first) & (lane < first + width), row, tiles[t])
    for t in range(TILES):
        packed_ref[t] = tiles[t]


def side_cells():
    cells = np.full((3, TILES * LANES, 1), -(1 << 20), np.int32)
    for r, (t, first, width) in PIECES.items():
        for c in range(width):
            cells[:, t * LANES + first + c, 0] = (r - HALO, c - width, LANES + c)
    return cells


def sources(place_ref, rates_ref, plan_ref, x_ref, y_ref, cells_ref, centre_ref, left_ref, right_ref):
    bores = plan_ref.shape[1]
    plan = plan_ref[...]
    rate = jnp.zeros(plan.shape, F32)
    for j in range(NPULSE):
        rate = jnp.where(plan == j, rates_ref[j], rate)
    rate = jnp.concatenate([rate, jnp.zeros((1, bores), F32)], axis=0)
    rate_high = rate.astype(BF16).astype(F32)
    rate_low = rate - rate_high
    x = x_ref[...] - place_ref[1] * ROWS
    y = y_ref[...] - place_ref[2] * LANES
    hit_x = x == lax.broadcasted_iota(jnp.int32, (ZS, bores), 0) - HALO
    hit_y = (y == lax.broadcasted_iota(jnp.int32, (LANES, bores), 0)).astype(F32).astype(BF16)
    contract = lambda p, q: lax.dot_general(p, q, (((1,), (1,)), ((), ())), preferred_element_type=F32)

    def plane(rates):
        left = [jnp.where(hit_x, rates[m : m + 1], 0.0) for m in range(STEPS + 1)]
        return contract(jnp.concatenate(left, axis=0).astype(BF16), hit_y)

    both = plane(rate_high) + plane(rate_low)
    for m in range(STEPS + 1):
        centre_ref[pl.ds(m, ZS, stride=8), :] = both[m * ZS : (m + 1) * ZS]
    centre_ref[pl.ds(7, ZS, stride=8), :] = jnp.zeros((ZS, LANES), F32)
    rates = jnp.concatenate([rate_high, rate_low], axis=0).astype(BF16)
    for side, ref in ((1, left_ref), (2, right_ref)):
        hit = (x == cells_ref[0]) & (y == cells_ref[side])
        both = contract(rates, hit.astype(F32).astype(BF16))
        ref[...] = both[:8] + both[8:]


def coefs(place_ref, lateral_ref, vertical_ref, ids_ref, out_ref, poly_ref):
    ids = jnp.broadcast_to(ids_ref[...], (8, LANES))
    lane = lax.broadcasted_iota(jnp.int32, (8, LANES), 1)
    cond, lat = jnp.zeros((8, LANES), F32), jnp.zeros((8, LANES), F32)
    for j in range(NLAYER):
        cond = jnp.where(ids == j, vertical_ref[j], cond)
        lat = jnp.where(ids == j, lateral_ref[j], lat)
    cond = jnp.where(lane < NZ, cond, 1.0)
    lat = jnp.where(lane < NZ, lat, 0.0)
    after = pltpu.roll(cond, LANES - 1, axis=1)
    link = jnp.where(lane < NZ - 1, 2.0 * cond * after / (cond + after), 0.0)
    before = pltpu.roll(link, 1, axis=1)
    low, up = -before, -link
    mid = 1.0 + (jnp.where(lane == 0, cond, 0.0) + link + before)
    mid = jnp.where(lane < NZ, mid, 1.0)
    row_id = lax.broadcasted_iota(jnp.int32, (NZ, LANES), 0)
    lane_id = lax.broadcasted_iota(jnp.int32, (NZ, LANES), 1)
    rhs = (row_id == lane_id).astype(F32)
    wide = lambda v: jnp.broadcast_to(v[:1], (NZ, LANES))
    for s in (1, 2, 4, 8, 16, 32):
        back = lambda v: pltpu.roll(v, s, axis=1)
        forth = lambda v: pltpu.roll(v, LANES - s, axis=1)
        alpha = -low / back(mid)
        gamma = -up / forth(mid)
        rhs = rhs + wide(alpha) * back(rhs) + wide(gamma) * forth(rhs)
        mid = mid + alpha * back(up) + gamma * forth(low)
        low, up = alpha * back(low), gamma * forth(up)
    inverse = rhs / wide(mid)
    inverse = jnp.concatenate([inverse, jnp.zeros((LANES - NZ, LANES), F32)], axis=0)
    high = inverse.astype(BF16).astype(F32)
    weights = high + pltpu.roll(inverse - high, 64, axis=1)
    weights = jnp.concatenate([weights, high], axis=0).astype(BF16)

    def solve(blocks):
        high, low = split(jnp.concatenate(blocks, axis=0))
        both = jnp.dot(jnp.concatenate([high, low], axis=1), weights, preferred_element_type=F32)
        return both + pltpu.roll(both, 64, axis=1)

    row_id = lax.broadcasted_iota(jnp.int32, (ZS, LANES), 0)
    lane_id = lax.broadcasted_iota(jnp.int32, (ZS, LANES), 1)
    eye = ((row_id == lane_id) & (row_id < NZ)).astype(F32)
    profile = (lane_id >= 2) & (lane_id < NZ - 4)
    source = [((row_id == NZ + n) & profile).astype(F32) for n in range(STEPS + 1)]
    slope = jnp.broadcast_to(lat[:1], (ZS, LANES))
    stay = 1.0 - 4.0 * slope

    degree = lambda p, n: 0 if n == 0 else n + p

    def get(p, n, k):
        if k > degree(p, n):
            return None
        return eye if n == 0 else poly_ref[p, n, k * ZS : (k + 1) * ZS, :]

    def total(*terms):
        terms = [(f, t) for f, t in terms if t is not None]
        result = None
        for f, t in terms:
            t = t if f in (1.0, -1.0) else f * t
            if result is None:
                result = -t if f == -1.0 else t
            else:
                result = result - t if f == -1.0 else result + t
        return result

    def step(p, n):
        count = degree(p, n + 1) + 1
        blocks, rest, last = [], [], None
        for k in range(count):
            if p == 0:
                g = get(0, n, k)
                tail, add = None, source[n]
            else:
                b, c = get(p - 1, n, k), get(p - 1, n + 1, k)
                if n == 0:
                    w = total((0.5, b), (0.5, c))
                    g, add = w, 0.5 * source[0] + 0.5 * source[1]
                else:
                    w = total((-1.0 / 12.0, get(p - 1, n - 1, k)), (8.0 / 12.0, b), (5.0 / 12.0, c))
                    g = total((1.0, get(p, n, k)), (-1.0, b), (1.0, w))
                    add = (-source[n - 1] + 8.0 * source[n] + 5.0 * source[n + 1]) * (1.0 / 12.0)
                tail = total((1.0, b), (-1.0, c))
                rest.append(total((1.0, c), (-1.0, w)))
            parts = [
                (1.0, None if g is None else stay * g),
                (1.0, None if last is None else slope * last),
                (1.0, tail),
                (1.0, add if k == 0 else None),
            ]
            blocks.append(total(*parts))
            last = g
        solved = solve(blocks)
        for k in range(count):
            block = solved[k * ZS : (k + 1) * ZS]
            if p > 0 and rest[k] is not None:
                block = block + rest[k]
            poly_ref[p, n + 1, k * ZS : (k + 1) * ZS, :] = block

    for p in range(LEVELS):
        first = (degree(p, STEPS) + 1) * ZS
        if first < POWERS * ZS:
            poly_ref[p, STEPS, first:, :] = jnp.zeros((POWERS * ZS - first, LANES), F32)
    for wave in range(STEPS + LEVELS - 1):
        for p in range(LEVELS):
            if 0 <= wave - p < STEPS:
                step(p, wave - p)

    level = place_ref[0]
    blank = jnp.zeros((SLOT - ZS, LANES), F32)
    for k in range(POWERS):
        block = poly_ref[level, STEPS, k * ZS : (k + 1) * ZS, :]
        block = jnp.concatenate([jnp.where(lane_id < NZ, block, 0.0), blank], axis=0)
        block = jnp.concatenate([block, pltpu.roll(block, SLOT, axis=1)], axis=0)
        high = block.astype(BF16).astype(F32)
        block = jnp.concatenate([high, block - high], axis=1).astype(BF16)
        out_ref[k, :LANES, :] = block
        out_ref[k, LANES:, :] = block


def evolve(
    place_ref, u_ref, above_ref, below_ref, own_ref, other_ref, src_centre_ref, src_left_ref, src_right_ref, coef_ref,
    out_ref, line_ref, side_ref, field_ref, other_field_ref, total_ref,
):
    level, tx, ty = place_ref[0], place_ref[1], place_ref[2]
    lane = lax.broadcasted_iota(jnp.int32, (BLOCKS, LANES), 1)
    sublane = lax.broadcasted_iota(jnp.int32, (BLOCKS, LANES), 0)
    blank = jnp.zeros((SLOT - ZS, LANES), F32)
    low_level = level < 2
    for t in range(TILES):
        own, other = own_ref[t], other_ref[t]
        part = slice(t * LANES, (t + 1) * LANES)
        left = [jnp.where(low_level, own, other), src_left_ref[:, part], blank]
        right = [jnp.where(low_level, other, own), src_right_ref[:, part], blank]
        side_ref[0, part, :] = jnp.concatenate(left + left, axis=0).T
        side_ref[1, part, :] = jnp.concatenate(right + right, axis=0).T

    def halo_of(side, r):
        t, first, width = PIECES.get(r, (0, 0, HALO))
        first = t * LANES + first + (width - HALO if side == 0 else 0)
        return side_ref[side, first : first + HALO, :]

    in_low_half = lax.broadcasted_iota(jnp.int32, (HALO, LANES), 1) < SLOT
    for i in range(PAIRS):
        rows = []
        for r in (i, i + HALF):
            rows += [ext_row(r, u_ref, above_ref, below_ref), src_centre_ref[8 * r : 8 * r + 8, :], blank]
        line_ref[i, HALO : HALO + LANES, :] = jnp.concatenate(rows, axis=0).T
        line_ref[i, :HALO, :] = jnp.where(in_low_half, halo_of(0, i), halo_of(0, i + HALF))
        right = jnp.where(in_low_half, halo_of(1, i), halo_of(1, i + HALF))
        line_ref[i, HALO + LANES : 2 * HALO + LANES, :] = right
        line_ref[i, 2 * HALO + LANES :, :] = jnp.zeros((WIDE - 2 * HALO - LANES, LANES), F32)
        for j in range(SPAN):
            field_ref[i, 8 * j : 8 * j + 8, :] = line_ref[i, pl.ds(j, BLOCKS, stride=SPAN), :]

    above = jnp.where((lane < SLOT) & (tx == 0), 0.0, 1.0)
    below = jnp.where((lane >= SLOT) & (tx == place_ref[3]), 0.0, 1.0)
    left = jnp.where((sublane == 0) & (ty == 0), 0.0, 1.0)
    right = jnp.where((sublane == BLOCKS - 1) & (ty == place_ref[4]), 0.0, 1.0)
    first_right = HALO + LANES - (BLOCKS - 1) * SPAN

    def advance(source, target, first, count, mask=None):
        left_in, right_in = (left, right) if mask is None else (left * mask, right * mask)
        load = lambda i, j: source[first + i, 8 * j : 8 * j + 8, :]
        for start in range(0, SPAN, CHUNK):
            inner = range(start, min(start + CHUNK, SPAN))
            before = [load(-1, j) for j in inner]
            centre = [load(0, j) for j in inner]
            for i in range(count):
                after = [load(i + 1, j) for j in inner]
                if start == 0:
                    low = pltpu.roll(load(i, SPAN - 1), 1, axis=0)
                else:
                    low = load(i, start - 1)
                if inner[-1] == SPAN - 1:
                    high = pltpu.roll(load(i, 0), BLOCKS - 1, axis=0)
                else:
                    high = load(i, inner[-1] + 1)
                line = [low] + centre + [high]
                for n, j in enumerate(inner):
                    new = (before[n] + after[n]) + (line[n] + line[n + 2])
                    if j < HALO:
                        new = new * (left_in if j < first_right else left_in * right)
                    else:
                        new = new * right_in
                    target[first + i, 8 * j : 8 * j + 8, :] = new
                before, centre = centre, after

    def collect(k, source):
        cells = source[HALO : HALO + HALF].reshape(HALF * WIDE, LANES)
        high, low = split(cells)
        both = jnp.dot(jnp.concatenate([high, low], axis=1), coef_ref[k], preferred_element_type=F32)
        both = (both[:, :LANES] + both[:, LANES:]).reshape(HALF, WIDE, LANES)
        total_ref[...] = both if k == 0 else total_ref[...] + both

    for k in range(POWERS):
        source, target = (field_ref, other_field_ref)[:: 1 if k % 2 == 0 else -1]

        collect(k, source)
        if k + 1 < POWERS:
            advance(source, target, HALO, HALF)
        if k + 1 < HALO:
            advance(source, target, k + 1, HALO - k - 1, above)
            advance(source, target, HALO + HALF, HALO - k - 1, below)

    for i in range(HALF):
        for j in range(SPAN):
            line_ref[i, pl.ds(j, BLOCKS, stride=SPAN), :] = total_ref[i, 8 * j : 8 * j + 8, :]
        result = line_ref[i, HALO : HALO + LANES, :].T
        out_ref[pl.ds(i, NZ, stride=ROWS), :] = result[:NZ]
        out_ref[pl.ds(i + HALF, NZ, stride=ROWS), :] = result[SLOT : SLOT + NZ]


SMEM = pl.BlockSpec(memory_space=pltpu.SMEM)
WHOLE = pl.BlockSpec(memory_space=pltpu.VMEM)


def call(kernel, name, ins, outs, scratch=(), cost=0):
    return pl.pallas_call(
        kernel,
        out_shape=outs,
        in_specs=ins,
        out_specs=jax.tree.map(lambda _: WHOLE, outs),
        scratch_shapes=list(scratch),
        compiler_params=pltpu.CompilerParams(vmem_limit_bytes=VMEM),
        cost_estimate=pl.CostEstimate(flops=cost, bytes_accessed=1 << 20, transcendentals=0),
        name=name,
    )


def on_device(initial, layer_ids, lateral_number, vertical_number, pulse_rates, bore_x, bore_y, plan):
    shape = lambda *s, dtype=F32: jax.ShapeDtypeStruct(s, dtype)
    count_x, count_y = lax.axis_size("tx"), lax.axis_size("ty")
    indices = [lax.axis_index(name) for name in ("level", "tx", "ty")]
    place = jnp.stack(indices + [jnp.int32(count_x - 1), jnp.int32(count_y - 1)])
    flat = initial.reshape(NZ * ROWS, LANES)
    slab = shape(HALO, NZ, LANES)
    top, bottom = call(edge_rows, "edge_rows", [WHOLE], (slab, slab))(flat)
    up = [(i, i + 1) for i in range(count_x - 1)]
    above = lax.ppermute(bottom, "tx", up)
    below = lax.ppermute(top, "tx", [(j, i) for i, j in up])
    strips = call(edge_columns, "edge_columns", [SMEM] + [WHOLE] * 3, shape(TILES, NZ, LANES))(
        place, flat, above, below
    )
    route = []
    for i in range(count_y - 1):
        for l in (0, 1):
            route.append(((l + 2) * count_y + i, l * count_y + i + 1))
            route.append((l * count_y + i + 1, (l + 2) * count_y + i))
    own = lax.ppermute(strips, ("level", "ty"), route)
    other = lax.ppermute(own, "level", [(0, 2), (2, 0), (1, 3), (3, 1)])

    sides = shape(8, TILES * LANES)
    src = call(sources, "sources", [SMEM] * 2 + [WHOLE] * 4, (shape(ZS * 8, LANES), sides, sides), cost=1 << 28)(
        place, pulse_rates, plan.T, bore_x[None, :], bore_y[None, :], side_cells()
    )
    ids = jnp.pad(layer_ids, (0, LANES - NZ))[None, :]
    table = call(
        coefs,
        "coefs",
        [SMEM] * 3 + [WHOLE],
        shape(POWERS, 2 * LANES, 2 * LANES, dtype=BF16),
        [pltpu.VMEM((LEVELS, STEPS + 1, POWERS * ZS, LANES), F32)],
        cost=1 << 28,
    )(place, lateral_number, vertical_number, ids)
    result = call(
        evolve,
        "evolve",
        [SMEM] + [WHOLE] * 9,
        shape(NZ * ROWS, LANES),
        [
            pltpu.VMEM((PAIRS, WIDE, LANES), F32),
            pltpu.VMEM((2, TILES * LANES, LANES), F32),
            pltpu.VMEM((PAIRS, WIDE, LANES), F32),
            pltpu.VMEM((PAIRS, WIDE, LANES), F32),
            pltpu.VMEM((HALF, WIDE, LANES), F32),
        ],
    )(place, flat, above, below, own, other, *src, table)
    return result.reshape(1, NZ, ROWS, LANES)


def solution(mesh):
    return jax.shard_map(
        on_device,
        mesh=mesh,
        in_specs=(P(None, "tx", "ty"), P(), P(), P(), P(), P(), P(), P()),
        out_specs=P("level", None, "tx", "ty"),
        check_vma=False,
    )
```

```python
import jax
import jax.numpy as jnp
import numpy as np
from jax import lax
from jax.experimental import pallas as pl
from jax.experimental.pallas import tpu as pltpu
from jax.sharding import PartitionSpec as P

NZ = 48
STEPS = 6
NLAYER = 6
NPULSE = 8
LEVELS = 4
POWERS = STEPS + LEVELS
HALO = POWERS - 1
ROWS = 32
LANES = 128
EXT = ROWS + 2 * HALO
ZS = NZ + 8
HALF = ROWS // 2
PAIRS = HALF + 2 * HALO
SLOT = LANES // 2
BLOCKS = 8
BACK = (POWERS - 1) // 2
SPAN = (LANES + 2 * BACK) // BLOCKS
RIM = 20
RIM_SPAN = 2 * RIM // BLOCKS
CHUNK = 5
VMEM = 48 * 1024 * 1024
F32, BF16 = jnp.float32, jnp.bfloat16


def pieces():
    width = [HALO - max(HALO - r, r - (HALO + ROWS - 1), 0) for r in range(EXT)]
    slots = [[r] for r in range(EXT) if width[r] == HALO]
    for d in range(1, (HALO + 1) // 2):
        slots.append([HALO - d, d])
        slots.append([EXT - 1 - (HALO - d), EXT - 1 - d])
    where, per_tile = {}, LANES // HALO
    for n, rows in enumerate(slots):
        lane = HALO * (n % per_tile)
        for r in rows:
            where[r] = (n // per_tile, lane, width[r])
            lane += width[r]
    return where, -(-len(slots) // per_tile)


PIECES, TILES = pieces()


def split(x):
    high = x.astype(BF16)
    return high, (x - high.astype(F32)).astype(BF16)


def edge_rows(place_ref, u_ref, far_ref, near_ref, kept_ref):
    even = lax.rem(place_ref[1], 2) == 0
    for i in range(HALO):
        first = u_ref[pl.ds(i, NZ, stride=ROWS), :]
        last = u_ref[pl.ds(ROWS - HALO + i, NZ, stride=ROWS), :]
        far_ref[i] = jnp.where(even, first, last)
        near_ref[i] = jnp.where(even, last, first)
    kept_ref[...] = u_ref[...]


def ext_row(r, even, u_ref, far_ref, near_ref):
    if r < HALO:
        return jnp.where(even, far_ref[r], near_ref[r])
    if r < HALO + ROWS:
        return u_ref[pl.ds(r - HALO, NZ, stride=ROWS), :]
    return jnp.where(even, near_ref[r - HALO - ROWS], far_ref[r - HALO - ROWS])


def pack(place_ref, rows, row_of, packed_ref, tiles):
    lane = lax.broadcasted_iota(jnp.int32, (NZ, LANES), 1)
    send_last = place_ref[0] >= 2
    for r in rows:
        t, first, width = PIECES[r]
        row = pltpu.roll(row_of(r), first + jnp.where(send_last, width, 0), axis=1)
        tiles[t] = jnp.where((lane >= first) & (lane < first + width), row, tiles[t])
    for t in range(TILES):
        packed_ref[t] = tiles[t]


def own_columns(place_ref, u_ref, packed_ref):
    row_of = lambda r: u_ref[pl.ds(r - HALO, NZ, stride=ROWS), :]
    pack(place_ref, range(HALO, HALO + ROWS), row_of, packed_ref, [jnp.zeros((NZ, LANES), F32)] * TILES)


def edge_columns(place_ref, strips_ref, far_ref, near_ref, packed_ref):
    even = lax.rem(place_ref[1], 2) == 0
    rows = [r for r in PIECES if not HALO <= r < HALO + ROWS]
    row_of = lambda r: ext_row(r, even, None, far_ref, near_ref)
    pack(place_ref, rows, row_of, packed_ref, [strips_ref[t] for t in range(TILES)])


def side_cells():
    cells = np.full((8, TILES * LANES), -(1 << 20), np.float32)
    for r, (t, first, width) in PIECES.items():
        for c in range(width):
            cells[:3, t * LANES + first + c] = (r - HALO, c - width, LANES + c)
    return cells


def sources(place_ref, rates_ref, plan_ref, x_ref, y_ref, cells_ref, centre_ref, left_ref, right_ref):
    bores = plan_ref.shape[1]
    plan = plan_ref[...]
    rate = jnp.zeros(plan.shape, F32)
    for j in range(NPULSE):
        rate = jnp.where(plan == j, rates_ref[j], rate)
    rate = jnp.concatenate([rate, jnp.zeros((1, bores), F32)], axis=0)
    rate_high = rate.astype(BF16).astype(F32)
    rate_low = rate - rate_high
    x = x_ref[...] - place_ref[1] * ROWS
    y = y_ref[...] - place_ref[2] * LANES
    hit_x = x == lax.broadcasted_iota(jnp.int32, (ZS, bores), 0) - HALO
    hit_y = (y == lax.broadcasted_iota(jnp.int32, (LANES, bores), 0)).astype(F32).astype(BF16)
    contract = lambda p, q: lax.dot_general(p, q, (((1,), (1,)), ((), ())), preferred_element_type=F32)

    def plane(rates):
        left = [jnp.where(hit_x, rates[m : m + 1], 0.0) for m in range(STEPS + 1)]
        return contract(jnp.concatenate(left, axis=0).astype(BF16), hit_y)

    both = plane(rate_high) + plane(rate_low)
    for m in range(STEPS + 1):
        centre_ref[pl.ds(m, ZS, stride=8), :] = both[m * ZS : (m + 1) * ZS]
    centre_ref[pl.ds(7, ZS, stride=8), :] = jnp.zeros((ZS, LANES), F32)
    rates = jnp.concatenate([rate_high, rate_low], axis=0).astype(BF16)
    columns = [cells_ref[:, t * LANES : (t + 1) * LANES].T for t in range(TILES)]
    columns = jnp.concatenate(columns, axis=0).astype(jnp.int32)
    for side, ref in ((1, left_ref), (2, right_ref)):
        hit = (x == columns[:, :1]) & (y == columns[:, side : side + 1])
        both = contract(rates, hit.astype(F32).astype(BF16))
        ref[...] = both[:8] + both[8:]


def coefs(place_ref, lateral_ref, vertical_ref, ids_ref, out_ref, poly_ref):
    ids = jnp.broadcast_to(ids_ref[...], (8, LANES))
    lane = lax.broadcasted_iota(jnp.int32, (8, LANES), 1)
    cond, lat = jnp.zeros((8, LANES), F32), jnp.zeros((8, LANES), F32)
    for j in range(NLAYER):
        cond = jnp.where(ids == j, vertical_ref[j], cond)
        lat = jnp.where(ids == j, lateral_ref[j], lat)
    cond = jnp.where(lane < NZ, cond, 1.0)
    lat = jnp.where(lane < NZ, lat, 0.0)
    after = pltpu.roll(cond, LANES - 1, axis=1)
    link = jnp.where(lane < NZ - 1, 2.0 * cond * after / (cond + after), 0.0)
    before = pltpu.roll(link, 1, axis=1)
    low, up = -before, -link
    mid = 1.0 + (jnp.where(lane == 0, cond, 0.0) + link + before)
    mid = jnp.where(lane < NZ, mid, 1.0)
    row_id = lax.broadcasted_iota(jnp.int32, (NZ, LANES), 0)
    lane_id = lax.broadcasted_iota(jnp.int32, (NZ, LANES), 1)
    rhs = (row_id == lane_id).astype(F32)
    wide = lambda v: jnp.broadcast_to(v[:1], (NZ, LANES))
    for s in (1, 2, 4, 8, 16, 32):
        back = lambda v: pltpu.roll(v, s, axis=1)
        forth = lambda v: pltpu.roll(v, LANES - s, axis=1)
        alpha = -low / back(mid)
        gamma = -up / forth(mid)
        rhs = rhs + wide(alpha) * back(rhs) + wide(gamma) * forth(rhs)
        mid = mid + alpha * back(up) + gamma * forth(low)
        low, up = alpha * back(low), gamma * forth(up)
    inverse = rhs / wide(mid)
    inverse = jnp.concatenate([inverse, jnp.zeros((LANES - NZ, LANES), F32)], axis=0)
    high = inverse.astype(BF16).astype(F32)
    weights = high + pltpu.roll(inverse - high, 64, axis=1)
    weights = jnp.concatenate([weights, high], axis=0).astype(BF16)

    def solve(blocks):
        high, low = split(jnp.concatenate(blocks, axis=0))
        both = jnp.dot(jnp.concatenate([high, low], axis=1), weights, preferred_element_type=F32)
        return both + pltpu.roll(both, 64, axis=1)

    row_id = lax.broadcasted_iota(jnp.int32, (ZS, LANES), 0)
    lane_id = lax.broadcasted_iota(jnp.int32, (ZS, LANES), 1)
    eye = ((row_id == lane_id) & (row_id < NZ)).astype(F32)
    profile = (lane_id >= 2) & (lane_id < NZ - 4)
    source = [((row_id == NZ + n) & profile).astype(F32) for n in range(STEPS + 1)]
    slope = jnp.broadcast_to(lat[:1], (ZS, LANES))
    stay = 1.0 - 4.0 * slope

    degree = lambda p, n: 0 if n == 0 else n + p

    def get(p, n, k):
        if k > degree(p, n):
            return None
        return eye if n == 0 else poly_ref[p, n, k * ZS : (k + 1) * ZS, :]

    def total(*terms):
        terms = [(f, t) for f, t in terms if t is not None]
        result = None
        for f, t in terms:
            t = t if f in (1.0, -1.0) else f * t
            if result is None:
                result = -t if f == -1.0 else t
            else:
                result = result - t if f == -1.0 else result + t
        return result

    def step(p, n):
        count = degree(p, n + 1) + 1
        blocks, rest, last = [], [], None
        for k in range(count):
            if p == 0:
                g = get(0, n, k)
                tail, add = None, source[n]
            else:
                b, c = get(p - 1, n, k), get(p - 1, n + 1, k)
                if n == 0:
                    w = total((0.5, b), (0.5, c))
                    g, add = w, 0.5 * source[0] + 0.5 * source[1]
                else:
                    w = total((-1.0 / 12.0, get(p - 1, n - 1, k)), (8.0 / 12.0, b), (5.0 / 12.0, c))
                    g = total((1.0, get(p, n, k)), (-1.0, b), (1.0, w))
                    add = (-source[n - 1] + 8.0 * source[n] + 5.0 * source[n + 1]) * (1.0 / 12.0)
                tail = total((1.0, b), (-1.0, c))
                rest.append(total((1.0, c), (-1.0, w)))
            parts = [
                (1.0, None if g is None else stay * g),
                (1.0, None if last is None else slope * last),
                (1.0, tail),
                (1.0, add if k == 0 else None),
            ]
            blocks.append(total(*parts))
            last = g
        solved = solve(blocks)
        for k in range(count):
            block = solved[k * ZS : (k + 1) * ZS]
            if p > 0 and rest[k] is not None:
                block = block + rest[k]
            poly_ref[p, n + 1, k * ZS : (k + 1) * ZS, :] = block

    for p in range(LEVELS):
        first = (degree(p, STEPS) + 1) * ZS
        if first < POWERS * ZS:
            poly_ref[p, STEPS, first:, :] = jnp.zeros((POWERS * ZS - first, LANES), F32)
    for wave in range(STEPS + LEVELS - 1):
        for p in range(LEVELS):
            if 0 <= wave - p < STEPS:
                step(p, wave - p)

    level = place_ref[0]
    blank = jnp.zeros((SLOT - ZS, LANES), F32)
    for k in range(POWERS):
        block = poly_ref[level, STEPS, k * ZS : (k + 1) * ZS, :]
        block = jnp.concatenate([jnp.where(lane_id < NZ, block, 0.0), blank], axis=0)
        block = jnp.concatenate([block, pltpu.roll(block, SLOT, axis=1)], axis=0)
        high = block.astype(BF16).astype(F32)
        block = jnp.concatenate([high, block - high], axis=1).astype(BF16)
        out_ref[k, :LANES, :] = block
        out_ref[k, LANES:, :] = block


def advance(source, target, span, first, count, edge=lambda j, new: new):
    load = lambda i, j: source[first + i, 8 * j : 8 * j + 8, :]
    sublane = lax.broadcasted_iota(jnp.int32, (BLOCKS, LANES), 0)
    for start in range(0, span, CHUNK):
        inner = range(start, min(start + CHUNK, span))
        before = [load(-1, j) for j in inner]
        centre = [load(0, j) for j in inner]
        for i in range(count):
            after = [load(i + 1, j) for j in inner]
            if start == 0:
                low = jnp.where(sublane == 0, 0.0, pltpu.roll(load(i, span - 1), 1, axis=0))
            else:
                low = load(i, start - 1)
            if inner[-1] == span - 1:
                high = jnp.where(sublane == BLOCKS - 1, 0.0, pltpu.roll(load(i, 0), BLOCKS - 1, axis=0))
            else:
                high = load(i, inner[-1] + 1)
            line = [low] + centre + [high]
            for n, j in enumerate(inner):
                new = (before[n] + after[n]) + (line[n] + line[n + 2])
                target[first + i, 8 * j : 8 * j + 8, :] = edge(j, new)
            before, centre = centre, after


def powers(fields, total_ref, coef_ref, span, edge, above, below):
    for k in range(POWERS):
        source, target = fields[k % 2], fields[1 - k % 2]
        cells = source[HALO : HALO + HALF].reshape(HALF * span * BLOCKS, LANES)
        high, low = split(cells)
        both = jnp.dot(jnp.concatenate([high, low], axis=1), coef_ref[k], preferred_element_type=F32)
        both = (both[:, :LANES] + both[:, LANES:]).reshape(HALF, span * BLOCKS, LANES)
        total_ref[...] = both if k == 0 else total_ref[...] + both
        if k + 1 < POWERS:
            advance(source, target, span, HALO, HALF, edge)
        if k + 1 < HALO:
            count = HALO - k - 1
            advance(source, target, span, k + 1, count, lambda j, new: edge(j, new) * above)
            advance(source, target, span, HALO + HALF, count, lambda j, new: edge(j, new) * below)


def grid_rows(place_ref):
    lane = lax.broadcasted_iota(jnp.int32, (BLOCKS, LANES), 1)
    above = jnp.where((lane < SLOT) & (place_ref[1] == 0), 0.0, 1.0)
    below = jnp.where((lane >= SLOT) & (place_ref[1] == place_ref[3]), 0.0, 1.0)
    return above, below


def bulk(
    place_ref, u_ref, far_ref, near_ref, src_ref, coef_ref, out_ref, line_ref, field_ref, other_field_ref, total_ref
):
    ty = place_ref[2]
    even = lax.rem(place_ref[1], 2) == 0
    sublane = lax.broadcasted_iota(jnp.int32, (BLOCKS, LANES), 0)
    blank = jnp.zeros((SLOT - ZS, LANES), F32)
    room = jnp.zeros((BACK, LANES), F32)
    for i in range(PAIRS):
        rows = []
        for r in (i, i + HALF):
            rows += [ext_row(r, even, u_ref, far_ref, near_ref), src_ref[8 * r : 8 * r + 8, :], blank]
        line_ref[i, :BACK, :] = room
        line_ref[i, BACK : BACK + LANES, :] = jnp.concatenate(rows, axis=0).T
        line_ref[i, BACK + LANES :, :] = room
        for j in range(SPAN):
            field_ref[i, 8 * j : 8 * j + 8, :] = line_ref[i, pl.ds(j, BLOCKS, stride=SPAN), :]
    left = jnp.where((sublane == 0) & (ty == 0), 0.0, 1.0)
    right = jnp.where((sublane == BLOCKS - 1) & (ty == place_ref[4]), 0.0, 1.0)

    def edge(j, new):
        return new * left if j < BACK else new * right if j >= SPAN - BACK else new

    powers((field_ref, other_field_ref), total_ref, coef_ref, SPAN, edge, *grid_rows(place_ref))
    for i in range(HALF):
        for j in range(SPAN):
            line_ref[i, pl.ds(j, BLOCKS, stride=SPAN), :] = total_ref[i, 8 * j : 8 * j + 8, :]
        out_ref[i] = line_ref[i, BACK : BACK + LANES, :]


def rim(
    place_ref, own_ref, other_ref, src_left_ref, src_right_ref, coef_ref, bulk_ref,
    out_ref, line_ref, side_ref, field_ref, other_field_ref, total_ref,
):
    low_level = place_ref[0] < 2
    blank = jnp.zeros((SLOT - ZS, LANES), F32)
    for side, src_ref in enumerate((src_left_ref, src_right_ref)):
        for t in range(TILES):
            part = slice(t * LANES, (t + 1) * LANES)
            tile = jnp.where(low_level == (side == 0), own_ref[t], other_ref[t])
            side_ref[side, part, :] = jnp.concatenate([tile, src_ref[:, part], blank] * 2, axis=0).T

    def halo_of(side, r):
        t, first, width = PIECES.get(r, (0, 0, HALO))
        first = t * LANES + first + (width - HALO if side == 0 else 0)
        return side_ref[side, first : first + HALO, :]

    in_low_half = lax.broadcasted_iota(jnp.int32, (HALO, LANES), 1) < SLOT
    room = jnp.zeros((2 * (RIM - HALO), LANES), F32)
    for i in range(PAIRS):
        line_ref[i, :HALO, :] = jnp.where(in_low_half, halo_of(0, i), halo_of(0, i + HALF))
        line_ref[i, HALO : 2 * RIM - HALO, :] = room
        line_ref[i, 2 * RIM - HALO :, :] = jnp.where(in_low_half, halo_of(1, i), halo_of(1, i + HALF))
        for j in range(RIM_SPAN):
            field_ref[i, 8 * j : 8 * j + 8, :] = line_ref[i, pl.ds(j, BLOCKS, stride=RIM_SPAN), :]
    powers((field_ref, other_field_ref), total_ref, coef_ref, RIM_SPAN, lambda j, new: new, *grid_rows(place_ref))
    for i in range(HALF):
        for j in range(RIM_SPAN):
            line_ref[i, pl.ds(j, BLOCKS, stride=RIM_SPAN), :] = total_ref[i, 8 * j : 8 * j + 8, :]
        inner = LANES - 2 * (RIM - HALO)
        change = [line_ref[i, HALO:RIM, :], jnp.zeros((inner, LANES), F32), line_ref[i, RIM : 2 * RIM - HALO, :]]
        result = (bulk_ref[i] + jnp.concatenate(change, axis=0)).T
        out_ref[pl.ds(i, NZ, stride=ROWS), :] = result[:NZ]
        out_ref[pl.ds(i + HALF, NZ, stride=ROWS), :] = result[SLOT : SLOT + NZ]


SMEM = pl.BlockSpec(memory_space=pltpu.SMEM)
WHOLE = pl.BlockSpec(memory_space=pltpu.VMEM)


def call(kernel, name, ins, outs, scratch=(), cost=0):
    return pl.pallas_call(
        kernel,
        out_shape=outs,
        in_specs=ins,
        out_specs=jax.tree.map(lambda _: WHOLE, outs),
        scratch_shapes=list(scratch),
        compiler_params=pltpu.CompilerParams(vmem_limit_bytes=VMEM),
        cost_estimate=pl.CostEstimate(flops=cost, bytes_accessed=1 << 20, transcendentals=0),
        name=name,
    )


def on_device(initial, layer_ids, lateral_number, vertical_number, pulse_rates, bore_x, bore_y, plan):
    shape = lambda *s, dtype=F32: jax.ShapeDtypeStruct(s, dtype)
    count_x, count_y = lax.axis_size("tx"), lax.axis_size("ty")
    indices = [lax.axis_index(name) for name in ("level", "tx", "ty")]
    place = jnp.stack(indices + [jnp.int32(count_x - 1), jnp.int32(count_y - 1)])
    flat = initial.reshape(NZ * ROWS, LANES)
    slab = shape(HALO, NZ, LANES)
    whole = shape(NZ * ROWS, LANES)
    far, near, kept = call(edge_rows, "edge_rows", [SMEM, WHOLE], (slab, slab, whole), cost=800 << 20)(place, flat)
    pairs = lambda first: [(i + a, i + 1 - a) for i in range(first, count_x - 1, 2) for a in (0, 1)]
    far = lax.ppermute(far, "tx", pairs(1))
    near = lax.ppermute(near, "tx", pairs(0))
    packed = shape(TILES, NZ, LANES)
    strips = call(own_columns, "own_columns", [SMEM, WHOLE], packed, cost=1000 << 20)(place, kept)
    sides = shape(8, TILES * LANES)
    src, src_left, src_right = call(
        sources, "sources", [SMEM] * 2 + [WHOLE] * 4, (shape(ZS * 8, LANES), sides, sides), cost=1700 << 20
    )(place, pulse_rates, plan.T, bore_x[None, :], bore_y[None, :], side_cells())
    strips, src = lax.optimization_barrier((strips, src))
    strips = call(edge_columns, "edge_columns", [SMEM] + [WHOLE] * 3, packed, cost=800 << 20)(
        place, strips, far, near
    )
    ids = jnp.pad(layer_ids, (0, LANES - NZ))[None, :]
    strips, ids = lax.optimization_barrier((strips, ids))
    route = []
    for i in range(count_y - 1):
        for l in (0, 1):
            route.append(((l + 2) * count_y + i, l * count_y + i + 1))
            route.append((l * count_y + i + 1, (l + 2) * count_y + i))
    own = lax.ppermute(strips, ("level", "ty"), route)
    table = call(
        coefs,
        "coefs",
        [SMEM] * 3 + [WHOLE],
        shape(POWERS, 2 * LANES, 2 * LANES, dtype=BF16),
        [pltpu.VMEM((LEVELS, STEPS + 1, POWERS * ZS, LANES), F32)],
        cost=4600 << 20,
    )(place, lateral_number, vertical_number, ids)
    own, table = lax.optimization_barrier((own, table))
    other = lax.ppermute(own, "level", [(0, 2), (2, 0), (1, 3), (3, 1)])
    room = lambda span: [pltpu.VMEM((PAIRS, span * BLOCKS, LANES), F32)]
    total = lambda span: [pltpu.VMEM((HALF, span * BLOCKS, LANES), F32)]
    inner = call(
        bulk,
        "bulk",
        [SMEM] + [WHOLE] * 5,
        shape(HALF, LANES, LANES),
        room(SPAN) * 3 + total(SPAN),
        cost=8000 << 20,
    )(place, kept, far, near, src, table)
    result = call(
        rim,
        "rim",
        [SMEM] + [WHOLE] * 6,
        whole,
        room(RIM_SPAN) + [pltpu.VMEM((2, TILES * LANES, LANES), F32)] + room(RIM_SPAN) * 2 + total(RIM_SPAN),
        cost=4000 << 20,
    )(place, own, other, src_left, src_right, table, inner)
    return result.reshape(1, NZ, ROWS, LANES)


def solution(mesh):
    return jax.shard_map(
        on_device,
        mesh=mesh,
        in_specs=(P(None, "tx", "ty"), P(), P(), P(), P(), P(), P(), P()),
        out_specs=P("level", None, "tx", "ty"),
        check_vma=False,
    )
```

```python
import jax
import jax.numpy as jnp
import numpy as np
from jax import lax
from jax.experimental import pallas as pl
from jax.experimental.pallas import tpu as pltpu
from jax.sharding import PartitionSpec as P

NZ = 48
STEPS = 6
NLAYER = 6
NPULSE = 8
LEVELS = 4
POWERS = STEPS + LEVELS
HALO = POWERS - 1
ROWS = 32
LANES = 128
EXT = ROWS + 2 * HALO
ZS = NZ + 8
HALF = ROWS // 2
PAIRS = HALF + 2 * HALO
SLOT = LANES // 2
BLOCKS = 8
BACK = (POWERS - 1) // 2
SPAN = (LANES + 2 * BACK) // BLOCKS
RIM = 20
RIM_SPAN = 2 * RIM // BLOCKS
CHUNK = 5
VMEM = 48 * 1024 * 1024
F32, BF16 = jnp.float32, jnp.bfloat16


def pieces():
    width = [HALO - max(HALO - r, r - (HALO + ROWS - 1), 0) for r in range(EXT)]
    slots = [[r] for r in range(EXT) if width[r] == HALO]
    for d in range(1, (HALO + 1) // 2):
        slots.append([HALO - d, d])
        slots.append([EXT - 1 - (HALO - d), EXT - 1 - d])
    where, per_tile = {}, LANES // HALO
    for n, rows in enumerate(slots):
        lane = HALO * (n % per_tile)
        for r in rows:
            where[r] = (n // per_tile, lane, width[r])
            lane += width[r]
    return where, -(-len(slots) // per_tile)


PIECES, TILES = pieces()


def split(x):
    high = x.astype(BF16)
    return high, (x - high.astype(F32)).astype(BF16)


def edge_rows(place_ref, u_ref, far_ref, near_ref, kept_ref):
    even = lax.rem(place_ref[1], 2) == 0
    for i in range(HALO):
        first = u_ref[pl.ds(i, NZ, stride=ROWS), :]
        last = u_ref[pl.ds(ROWS - HALO + i, NZ, stride=ROWS), :]
        far_ref[i] = jnp.where(even, first, last)
        near_ref[i] = jnp.where(even, last, first)
    kept_ref[...] = u_ref[...]


def ext_row(r, even, u_ref, far_ref, near_ref):
    if r < HALO:
        return jnp.where(even, far_ref[r], near_ref[r])
    if r < HALO + ROWS:
        return u_ref[pl.ds(r - HALO, NZ, stride=ROWS), :]
    return jnp.where(even, near_ref[r - HALO - ROWS], far_ref[r - HALO - ROWS])


def pack(place_ref, rows, row_of, packed_ref, tiles):
    lane = lax.broadcasted_iota(jnp.int32, (NZ, LANES), 1)
    send_last = place_ref[0] >= 2
    for r in rows:
        t, first, width = PIECES[r]
        row = pltpu.roll(row_of(r), first + jnp.where(send_last, width, 0), axis=1)
        tiles[t] = jnp.where((lane >= first) & (lane < first + width), row, tiles[t])
    for t in range(TILES):
        packed_ref[t] = tiles[t]


def own_columns(place_ref, u_ref, packed_ref):
    row_of = lambda r: u_ref[pl.ds(r - HALO, NZ, stride=ROWS), :]
    pack(place_ref, range(HALO, HALO + ROWS), row_of, packed_ref, [jnp.zeros((NZ, LANES), F32)] * TILES)


def edge_columns(place_ref, strips_ref, far_ref, near_ref, packed_ref):
    even = lax.rem(place_ref[1], 2) == 0
    rows = [r for r in PIECES if not HALO <= r < HALO + ROWS]
    row_of = lambda r: ext_row(r, even, None, far_ref, near_ref)
    pack(place_ref, rows, row_of, packed_ref, [strips_ref[t] for t in range(TILES)])


def side_cells():
    cells = np.full((8, TILES * LANES), -(1 << 20), np.float32)
    for r, (t, first, width) in PIECES.items():
        for c in range(width):
            cells[:3, t * LANES + first + c] = (r - HALO, c - width, LANES + c)
    return cells


def sources(place_ref, rates_ref, plan_ref, x_ref, y_ref, cells_ref, centre_ref, left_ref, right_ref):
    bores = plan_ref.shape[1]
    plan = plan_ref[...]
    rate = jnp.zeros(plan.shape, F32)
    for j in range(NPULSE):
        rate = jnp.where(plan == j, rates_ref[j], rate)
    rate = jnp.concatenate([rate, jnp.zeros((1, bores), F32)], axis=0)
    rate_high = rate.astype(BF16).astype(F32)
    rate_low = rate - rate_high
    x = x_ref[...] - place_ref[1] * ROWS
    y = y_ref[...] - place_ref[2] * LANES
    hit_x = x == lax.broadcasted_iota(jnp.int32, (ZS, bores), 0) - HALO
    hit_y = (y == lax.broadcasted_iota(jnp.int32, (LANES, bores), 0)).astype(F32).astype(BF16)
    contract = lambda p, q: lax.dot_general(p, q, (((1,), (1,)), ((), ())), preferred_element_type=F32)

    def plane(rates):
        left = [jnp.where(hit_x, rates[m : m + 1], 0.0) for m in range(STEPS + 1)]
        return contract(jnp.concatenate(left, axis=0).astype(BF16), hit_y)

    both = plane(rate_high) + plane(rate_low)
    for m in range(STEPS + 1):
        centre_ref[pl.ds(m, ZS, stride=8), :] = both[m * ZS : (m + 1) * ZS]
    centre_ref[pl.ds(7, ZS, stride=8), :] = jnp.zeros((ZS, LANES), F32)
    rates = jnp.concatenate([rate_high, rate_low], axis=0).astype(BF16)
    columns = [cells_ref[:, t * LANES : (t + 1) * LANES].T for t in range(TILES)]
    columns = jnp.concatenate(columns, axis=0).astype(jnp.int32)
    for side, ref in ((1, left_ref), (2, right_ref)):
        hit = (x == columns[:, :1]) & (y == columns[:, side : side + 1])
        both = contract(rates, hit.astype(F32).astype(BF16))
        ref[...] = both[:8] + both[8:]


def coefs(place_ref, lateral_ref, vertical_ref, ids_ref, out_ref, poly_ref):
    ids = jnp.broadcast_to(ids_ref[...], (8, LANES))
    lane = lax.broadcasted_iota(jnp.int32, (8, LANES), 1)
    cond, lat = jnp.zeros((8, LANES), F32), jnp.zeros((8, LANES), F32)
    for j in range(NLAYER):
        cond = jnp.where(ids == j, vertical_ref[j], cond)
        lat = jnp.where(ids == j, lateral_ref[j], lat)
    cond = jnp.where(lane < NZ, cond, 1.0)
    lat = jnp.where(lane < NZ, lat, 0.0)
    after = pltpu.roll(cond, LANES - 1, axis=1)
    link = jnp.where(lane < NZ - 1, 2.0 * cond * after / (cond + after), 0.0)
    before = pltpu.roll(link, 1, axis=1)
    low, up = -before, -link
    mid = 1.0 + (jnp.where(lane == 0, cond, 0.0) + link + before)
    mid = jnp.where(lane < NZ, mid, 1.0)
    row_id = lax.broadcasted_iota(jnp.int32, (NZ, LANES), 0)
    lane_id = lax.broadcasted_iota(jnp.int32, (NZ, LANES), 1)
    rhs = (row_id == lane_id).astype(F32)
    wide = lambda v: jnp.broadcast_to(v[:1], (NZ, LANES))
    for s in (1, 2, 4, 8, 16, 32):
        back = lambda v: pltpu.roll(v, s, axis=1)
        forth = lambda v: pltpu.roll(v, LANES - s, axis=1)
        alpha = -low / back(mid)
        gamma = -up / forth(mid)
        rhs = rhs + wide(alpha) * back(rhs) + wide(gamma) * forth(rhs)
        mid = mid + alpha * back(up) + gamma * forth(low)
        low, up = alpha * back(low), gamma * forth(up)
    inverse = rhs / wide(mid)
    inverse = jnp.concatenate([inverse, jnp.zeros((LANES - NZ, LANES), F32)], axis=0)
    high = inverse.astype(BF16).astype(F32)
    weights = jnp.concatenate([high, inverse - high], axis=1)
    weights = jnp.concatenate([weights, weights], axis=0).astype(BF16)

    def solve(blocks):
        high, low = split(jnp.concatenate(blocks, axis=0))
        both = jnp.dot(jnp.concatenate([high, low], axis=1), weights, preferred_element_type=F32)
        return both[:, :LANES] + both[:, LANES:]

    row_id = lax.broadcasted_iota(jnp.int32, (ZS, LANES), 0)
    lane_id = lax.broadcasted_iota(jnp.int32, (ZS, LANES), 1)
    eye = ((row_id == lane_id) & (row_id < NZ)).astype(F32)
    profile = (lane_id >= 2) & (lane_id < NZ - 4)
    source = [((row_id == NZ + n) & profile).astype(F32) for n in range(STEPS + 1)]
    slope = jnp.broadcast_to(lat[:1], (ZS, LANES))

    degree = lambda p, n: 0 if n == 0 else n + p

    def get(p, n, k):
        if k > degree(p, n):
            return None
        return eye if n == 0 else poly_ref[p, n, k * ZS : (k + 1) * ZS, :]

    def total(*terms):
        terms = [(f, t) for f, t in terms if t is not None]
        result = None
        for f, t in terms:
            t = t if f in (1.0, -1.0) else f * t
            if result is None:
                result = -t if f == -1.0 else t
            else:
                result = result - t if f == -1.0 else result + t
        return result

    def step(p, n):
        count = degree(p, n + 1) + 1
        blocks, rest, last = [], [], None
        for k in range(count):
            u = get(p, n, k)
            if p == 0:
                kept, g, add = u, u, source[n]
            else:
                b, c = get(p - 1, n, k), get(p - 1, n + 1, k)
                if n == 0:
                    q = total((0.5, c), (-0.5, b))
                    add = 0.5 * source[0] + 0.5 * source[1]
                else:
                    q = total((7.0 / 12.0, c), (-8.0 / 12.0, b), (1.0 / 12.0, get(p - 1, n - 1, k)))
                    add = (-source[n - 1] + 8.0 * source[n] + 5.0 * source[n + 1]) * (1.0 / 12.0)
                kept = total((1.0, u), (-1.0, q))
                g = total((1.0, kept), (1.0, c), (-1.0, b))
                rest.append(q)
            spread = total((1.0, last), (-4.0, g))
            blocks.append(total((1.0, kept), (1.0, None if spread is None else slope * spread), (1.0, add if k == 0 else None)))
            last = g
        solved = solve(blocks)
        for k in range(count):
            block = solved[k * ZS : (k + 1) * ZS]
            if p > 0 and rest[k] is not None:
                block = block + rest[k]
            poly_ref[p, n + 1, k * ZS : (k + 1) * ZS, :] = block

    for p in range(LEVELS):
        first = (degree(p, STEPS) + 1) * ZS
        if first < POWERS * ZS:
            poly_ref[p, STEPS, first:, :] = jnp.zeros((POWERS * ZS - first, LANES), F32)
    for wave in range(STEPS + LEVELS - 1):
        for p in range(LEVELS):
            if 0 <= wave - p < STEPS:
                step(p, wave - p)

    level = place_ref[0]
    blank = jnp.zeros((SLOT - ZS, LANES), F32)
    for k in range(POWERS):
        block = poly_ref[level, STEPS, k * ZS : (k + 1) * ZS, :]
        block = jnp.concatenate([jnp.where(lane_id < NZ, block, 0.0), blank], axis=0)
        block = jnp.concatenate([block, pltpu.roll(block, SLOT, axis=1)], axis=0)
        high = block.astype(BF16).astype(F32)
        block = jnp.concatenate([high, block - high], axis=1).astype(BF16)
        out_ref[k, :LANES, :] = block
        out_ref[k, LANES:, :] = block


def advance(source, target, span, first, count, edge=lambda j, new: new):
    load = lambda i, j: source[first + i, 8 * j : 8 * j + 8, :]
    sublane = lax.broadcasted_iota(jnp.int32, (BLOCKS, LANES), 0)
    for start in range(0, span, CHUNK):
        inner = range(start, min(start + CHUNK, span))
        before = [load(-1, j) for j in inner]
        centre = [load(0, j) for j in inner]
        for i in range(count):
            after = [load(i + 1, j) for j in inner]
            if start == 0:
                low = jnp.where(sublane == 0, 0.0, pltpu.roll(load(i, span - 1), 1, axis=0))
            else:
                low = load(i, start - 1)
            if inner[-1] == span - 1:
                high = jnp.where(sublane == BLOCKS - 1, 0.0, pltpu.roll(load(i, 0), BLOCKS - 1, axis=0))
            else:
                high = load(i, inner[-1] + 1)
            line = [low] + centre + [high]
            for n, j in enumerate(inner):
                new = (before[n] + after[n]) + (line[n] + line[n + 2])
                target[first + i, 8 * j : 8 * j + 8, :] = edge(j, new)
            before, centre = centre, after


def powers(fields, total_ref, coef_ref, span, edge, above, below):
    for k in range(POWERS):
        source, target = fields[k % 2], fields[1 - k % 2]
        cells = source[HALO : HALO + HALF].reshape(HALF * span * BLOCKS, LANES)
        high, low = split(cells)
        both = jnp.dot(jnp.concatenate([high, low], axis=1), coef_ref[k], preferred_element_type=F32)
        both = (both[:, :LANES] + both[:, LANES:]).reshape(HALF, span * BLOCKS, LANES)
        total_ref[...] = both if k == 0 else total_ref[...] + both
        if k + 1 < POWERS:
            advance(source, target, span, HALO, HALF, edge)
        if k + 1 < HALO:
            count = HALO - k - 1
            advance(source, target, span, k + 1, count, lambda j, new: edge(j, new) * above)
            advance(source, target, span, HALO + HALF, count, lambda j, new: edge(j, new) * below)


def grid_rows(place_ref):
    lane = lax.broadcasted_iota(jnp.int32, (BLOCKS, LANES), 1)
    above = jnp.where((lane < SLOT) & (place_ref[1] == 0), 0.0, 1.0)
    below = jnp.where((lane >= SLOT) & (place_ref[1] == place_ref[3]), 0.0, 1.0)
    return above, below


def bulk(
    place_ref, u_ref, far_ref, near_ref, src_ref, coef_ref, out_ref, line_ref, field_ref, other_field_ref, total_ref
):
    ty = place_ref[2]
    even = lax.rem(place_ref[1], 2) == 0
    sublane = lax.broadcasted_iota(jnp.int32, (BLOCKS, LANES), 0)
    blank = jnp.zeros((SLOT - ZS, LANES), F32)
    room = jnp.zeros((BACK, LANES), F32)
    for i in range(PAIRS):
        rows = []
        for r in (i, i + HALF):
            rows += [ext_row(r, even, u_ref, far_ref, near_ref), src_ref[8 * r : 8 * r + 8, :], blank]
        line_ref[i, :BACK, :] = room
        line_ref[i, BACK : BACK + LANES, :] = jnp.concatenate(rows, axis=0).T
        line_ref[i, BACK + LANES :, :] = room
        for j in range(SPAN):
            field_ref[i, 8 * j : 8 * j + 8, :] = line_ref[i, pl.ds(j, BLOCKS, stride=SPAN), :]
    left = jnp.where((sublane == 0) & (ty == 0), 0.0, 1.0)
    right = jnp.where((sublane == BLOCKS - 1) & (ty == place_ref[4]), 0.0, 1.0)

    def edge(j, new):
        return new * left if j < BACK else new * right if j >= SPAN - BACK else new

    powers((field_ref, other_field_ref), total_ref, coef_ref, SPAN, edge, *grid_rows(place_ref))
    for i in range(HALF):
        for j in range(SPAN):
            line_ref[i, pl.ds(j, BLOCKS, stride=SPAN), :] = total_ref[i, 8 * j : 8 * j + 8, :]
        out_ref[i] = line_ref[i, BACK : BACK + LANES, :]


def rim(
    place_ref, own_ref, other_ref, src_left_ref, src_right_ref, coef_ref, bulk_ref,
    out_ref, line_ref, side_ref, field_ref, other_field_ref, total_ref, result_ref, sems,
):
    low_level = place_ref[0] < 2
    blank = jnp.zeros((SLOT - ZS, LANES), F32)
    for side, src_ref in enumerate((src_left_ref, src_right_ref)):
        for t in range(TILES):
            part = slice(t * LANES, (t + 1) * LANES)
            tile = jnp.where(low_level == (side == 0), own_ref[t], other_ref[t])
            side_ref[side, part, :] = jnp.concatenate([tile, src_ref[:, part], blank] * 2, axis=0).T

    def halo_of(side, r):
        t, first, width = PIECES.get(r, (0, 0, HALO))
        first = t * LANES + first + (width - HALO if side == 0 else 0)
        return side_ref[side, first : first + HALO, :]

    in_low_half = lax.broadcasted_iota(jnp.int32, (HALO, LANES), 1) < SLOT
    room = jnp.zeros((2 * (RIM - HALO), LANES), F32)
    for i in range(PAIRS):
        line_ref[i, :HALO, :] = jnp.where(in_low_half, halo_of(0, i), halo_of(0, i + HALF))
        line_ref[i, HALO : 2 * RIM - HALO, :] = room
        line_ref[i, 2 * RIM - HALO :, :] = jnp.where(in_low_half, halo_of(1, i), halo_of(1, i + HALF))
        for j in range(RIM_SPAN):
            field_ref[i, 8 * j : 8 * j + 8, :] = line_ref[i, pl.ds(j, BLOCKS, stride=RIM_SPAN), :]
    powers((field_ref, other_field_ref), total_ref, coef_ref, RIM_SPAN, lambda j, new: new, *grid_rows(place_ref))
    copies = []
    for i in range(HALF):
        for j in range(RIM_SPAN):
            line_ref[i, pl.ds(j, BLOCKS, stride=RIM_SPAN), :] = total_ref[i, 8 * j : 8 * j + 8, :]
        inner = LANES - 2 * (RIM - HALO)
        change = [line_ref[i, HALO:RIM, :], jnp.zeros((inner, LANES), F32), line_ref[i, RIM : 2 * RIM - HALO, :]]
        result = (bulk_ref[i] + jnp.concatenate(change, axis=0)).T
        group, row = divmod(i, 8)
        result_ref[group, pl.ds(row, NZ, stride=8), :] = result[:NZ]
        result_ref[group + 2, pl.ds(row, NZ, stride=8), :] = result[SLOT : SLOT + NZ]
        if row == 7:
            for g in (group, group + 2):
                copies.append(pltpu.make_async_copy(result_ref.at[g].reshape(NZ, 8, LANES), out_ref.at[:, pl.ds(8 * g, 8), :], sems.at[g]))
                copies[-1].start()
    for copy in copies:
        copy.wait()


SMEM = pl.BlockSpec(memory_space=pltpu.SMEM)
WHOLE = pl.BlockSpec(memory_space=pltpu.VMEM)


def call(kernel, name, ins, outs, scratch=(), cost=0, out_spec=None):
    return pl.pallas_call(
        kernel,
        out_shape=outs,
        in_specs=ins,
        out_specs=out_spec or jax.tree.map(lambda _: WHOLE, outs),
        scratch_shapes=list(scratch),
        compiler_params=pltpu.CompilerParams(vmem_limit_bytes=VMEM),
        cost_estimate=pl.CostEstimate(flops=cost, bytes_accessed=1 << 20, transcendentals=0),
        name=name,
    )


def on_device(initial, layer_ids, lateral_number, vertical_number, pulse_rates, bore_x, bore_y, plan):
    shape = lambda *s, dtype=F32: jax.ShapeDtypeStruct(s, dtype)
    count_x, count_y = lax.axis_size("tx"), lax.axis_size("ty")
    indices = [lax.axis_index(name) for name in ("level", "tx", "ty")]
    place = jnp.stack(indices + [jnp.int32(count_x - 1), jnp.int32(count_y - 1)])
    flat = initial.reshape(NZ * ROWS, LANES)
    slab = shape(HALO, NZ, LANES)
    whole = shape(NZ * ROWS, LANES)
    far, near, kept = call(edge_rows, "edge_rows", [SMEM, WHOLE], (slab, slab, whole), cost=800 << 20)(place, flat)
    pairs = lambda first: [(i + a, i + 1 - a) for i in range(first, count_x - 1, 2) for a in (0, 1)]
    far = lax.ppermute(far, "tx", pairs(1))
    near = lax.ppermute(near, "tx", pairs(0))
    packed = shape(TILES, NZ, LANES)
    strips = call(own_columns, "own_columns", [SMEM, WHOLE], packed, cost=1000 << 20)(place, kept)
    sides = shape(8, TILES * LANES)
    src, src_left, src_right = call(
        sources, "sources", [SMEM] * 2 + [WHOLE] * 4, (shape(ZS * 8, LANES), sides, sides), cost=1700 << 20
    )(place, pulse_rates, plan.T, bore_x[None, :], bore_y[None, :], side_cells())
    strips, src = lax.optimization_barrier((strips, src))
    strips = call(edge_columns, "edge_columns", [SMEM] + [WHOLE] * 3, packed, cost=800 << 20)(
        place, strips, far, near
    )
    ids = jnp.pad(layer_ids, (0, LANES - NZ))[None, :]
    strips, ids = lax.optimization_barrier((strips, ids))
    route = []
    for i in range(count_y - 1):
        for l in (0, 1):
            route.append(((l + 2) * count_y + i, l * count_y + i + 1))
            route.append((l * count_y + i + 1, (l + 2) * count_y + i))
    own = lax.ppermute(strips, ("level", "ty"), route)
    table = call(
        coefs,
        "coefs",
        [SMEM] * 3 + [WHOLE],
        shape(POWERS, 2 * LANES, 2 * LANES, dtype=BF16),
        [pltpu.VMEM((LEVELS, STEPS + 1, POWERS * ZS, LANES), F32)],
        cost=4600 << 20,
    )(place, lateral_number, vertical_number, ids)
    own, table = lax.optimization_barrier((own, table))
    other = lax.ppermute(own, "level", [(0, 2), (2, 0), (1, 3), (3, 1)])
    room = lambda span: [pltpu.VMEM((PAIRS, span * BLOCKS, LANES), F32)]
    total = lambda span: [pltpu.VMEM((HALF, span * BLOCKS, LANES), F32)]
    inner = call(
        bulk,
        "bulk",
        [SMEM] + [WHOLE] * 5,
        shape(HALF, LANES, LANES),
        room(SPAN) * 3 + total(SPAN),
        cost=8000 << 20,
    )(place, kept, far, near, src, table)
    result = call(
        rim,
        "rim",
        [SMEM] + [WHOLE] * 6,
        shape(NZ, ROWS, LANES),
        room(RIM_SPAN)
        + [pltpu.VMEM((2, TILES * LANES, LANES), F32)]
        + room(RIM_SPAN) * 2
        + total(RIM_SPAN)
        + [pltpu.VMEM((ROWS // 8, NZ * 8, LANES), F32), pltpu.SemaphoreType.DMA((ROWS // 8,))],
        out_spec=pl.BlockSpec(memory_space=pl.ANY),
        cost=4000 << 20,
    )(place, own, other, src_left, src_right, table, inner)
    return result.reshape(1, NZ, ROWS, LANES)


def solution(mesh):
    return jax.shard_map(
        on_device,
        mesh=mesh,
        in_specs=(P(None, "tx", "ty"), P(), P(), P(), P(), P(), P(), P()),
        out_specs=P("level", None, "tx", "ty"),
        check_vma=False,
    )
```

```python
import jax
import jax.numpy as jnp
import numpy as np
from jax import lax
from jax.experimental import pallas as pl
from jax.experimental.pallas import tpu as pltpu
from jax.sharding import PartitionSpec as P

NZ = 48
STEPS = 6
NLAYER = 6
NPULSE = 8
LEVELS = 4
POWERS = STEPS + LEVELS
HALO = POWERS - 1
ROWS = 32
LANES = 128
EXT = ROWS + 2 * HALO
ZS = NZ + 8
HALF = ROWS // 2
PAIRS = HALF + 2 * HALO
SLOT = LANES // 2
LINE = 4
BLOCKS = 8
BACK = (POWERS - 1) // 2
SPAN = (LANES + 2 * BACK) // BLOCKS
RIM = 20
RIM_SPAN = 2 * RIM // BLOCKS
CHUNK = 5
VMEM = 48 * 1024 * 1024
F32, BF16 = jnp.float32, jnp.bfloat16


def pieces():
    width = [HALO - max(HALO - r, r - (HALO + ROWS - 1), 0) for r in range(EXT)]
    slots = [[r] for r in range(EXT) if width[r] == HALO]
    for d in range(1, (HALO + 1) // 2):
        slots.append([HALO - d, d])
        slots.append([EXT - 1 - (HALO - d), EXT - 1 - d])
    where, per_tile = {}, LANES // HALO
    for n, rows in enumerate(slots):
        lane = HALO * (n % per_tile)
        for r in rows:
            where[r] = (n // per_tile, lane, width[r])
            lane += width[r]
    return where, -(-len(slots) // per_tile)


PIECES, TILES = pieces()


def split(x):
    high = x.astype(BF16)
    return high, (x - high.astype(F32)).astype(BF16)


def edge_rows(place_ref, u_ref, far_ref, near_ref, kept_ref):
    even = lax.rem(place_ref[1], 2) == 0
    for i in range(HALO):
        first = u_ref[pl.ds(i, NZ, stride=ROWS), :]
        last = u_ref[pl.ds(ROWS - HALO + i, NZ, stride=ROWS), :]
        far_ref[i] = jnp.where(even, first, last)
        near_ref[i] = jnp.where(even, last, first)
    kept_ref[...] = u_ref[...]


def ext_row(r, even, u_ref, far_ref, near_ref):
    if r < HALO:
        return jnp.where(even, far_ref[r], near_ref[r])
    if r < HALO + ROWS:
        return u_ref[pl.ds(r - HALO, NZ, stride=ROWS), :]
    return jnp.where(even, near_ref[r - HALO - ROWS], far_ref[r - HALO - ROWS])


def pack(place_ref, rows, row_of, packed_ref, tiles):
    lane = lax.broadcasted_iota(jnp.int32, (NZ, LANES), 1)
    send_last = place_ref[0] >= 2
    for r in rows:
        t, first, width = PIECES[r]
        row = pltpu.roll(row_of(r), first + jnp.where(send_last, width, 0), axis=1)
        tiles[t] = jnp.where((lane >= first) & (lane < first + width), row, tiles[t])
    for t in range(TILES):
        packed_ref[t] = tiles[t]


def own_columns(place_ref, u_ref, packed_ref):
    row_of = lambda r: u_ref[pl.ds(r - HALO, NZ, stride=ROWS), :]
    pack(place_ref, range(HALO, HALO + ROWS), row_of, packed_ref, [jnp.zeros((NZ, LANES), F32)] * TILES)


def edge_columns(place_ref, strips_ref, far_ref, near_ref, packed_ref):
    even = lax.rem(place_ref[1], 2) == 0
    rows = [r for r in PIECES if not HALO <= r < HALO + ROWS]
    row_of = lambda r: ext_row(r, even, None, far_ref, near_ref)
    pack(place_ref, rows, row_of, packed_ref, [strips_ref[t] for t in range(TILES)])


def side_cells():
    cells = np.full((8, TILES * LANES), -(1 << 20), np.float32)
    for r, (t, first, width) in PIECES.items():
        for c in range(width):
            cells[:3, t * LANES + first + c] = (r - HALO, c - width, LANES + c)
    return cells


def is_late(place_ref):
    return lax.rem(place_ref[2], LINE) == LINE - 1


def early_sources(place_ref, *refs):
    pl.when(jnp.logical_not(is_late(place_ref)))(lambda: sources(place_ref, *refs))


def sources(place_ref, rates_ref, plan_ref, x_ref, y_ref, cells_ref, centre_ref, left_ref, right_ref):
    bores = plan_ref.shape[1]
    plan = plan_ref[...]
    rate = jnp.zeros(plan.shape, F32)
    for j in range(NPULSE):
        rate = jnp.where(plan == j, rates_ref[j], rate)
    rate = jnp.concatenate([rate, jnp.zeros((1, bores), F32)], axis=0)
    rate_high = rate.astype(BF16).astype(F32)
    rate_low = rate - rate_high
    x = x_ref[...] - place_ref[1] * ROWS
    y = y_ref[...] - place_ref[2] * LANES
    hit_x = x == lax.broadcasted_iota(jnp.int32, (ZS, bores), 0) - HALO
    hit_y = (y == lax.broadcasted_iota(jnp.int32, (LANES, bores), 0)).astype(F32).astype(BF16)
    contract = lambda p, q: lax.dot_general(p, q, (((1,), (1,)), ((), ())), preferred_element_type=F32)

    def plane(rates):
        left = [jnp.where(hit_x, rates[m : m + 1], 0.0) for m in range(STEPS + 1)]
        return contract(jnp.concatenate(left, axis=0).astype(BF16), hit_y)

    both = plane(rate_high) + plane(rate_low)
    for m in range(STEPS + 1):
        centre_ref[pl.ds(m, ZS, stride=8), :] = both[m * ZS : (m + 1) * ZS]
    centre_ref[pl.ds(7, ZS, stride=8), :] = jnp.zeros((ZS, LANES), F32)
    rates = jnp.concatenate([rate_high, rate_low], axis=0).astype(BF16)
    columns = [cells_ref[:, t * LANES : (t + 1) * LANES].T for t in range(TILES)]
    columns = jnp.concatenate(columns, axis=0).astype(jnp.int32)
    for side, ref in ((1, left_ref), (2, right_ref)):
        hit = (x == columns[:, :1]) & (y == columns[:, side : side + 1])
        both = contract(rates, hit.astype(F32).astype(BF16))
        ref[...] = both[:8] + both[8:]


def coefs(place_ref, lateral_ref, vertical_ref, ids_ref, out_ref, poly_ref):
    ids = jnp.broadcast_to(ids_ref[...], (8, LANES))
    lane = lax.broadcasted_iota(jnp.int32, (8, LANES), 1)
    cond, lat = jnp.zeros((8, LANES), F32), jnp.zeros((8, LANES), F32)
    for j in range(NLAYER):
        cond = jnp.where(ids == j, vertical_ref[j], cond)
        lat = jnp.where(ids == j, lateral_ref[j], lat)
    cond = jnp.where(lane < NZ, cond, 1.0)
    lat = jnp.where(lane < NZ, lat, 0.0)
    after = pltpu.roll(cond, LANES - 1, axis=1)
    link = jnp.where(lane < NZ - 1, 2.0 * cond * after / (cond + after), 0.0)
    before = pltpu.roll(link, 1, axis=1)
    low, up = -before, -link
    mid = 1.0 + (jnp.where(lane == 0, cond, 0.0) + link + before)
    mid = jnp.where(lane < NZ, mid, 1.0)
    row_id = lax.broadcasted_iota(jnp.int32, (NZ, LANES), 0)
    lane_id = lax.broadcasted_iota(jnp.int32, (NZ, LANES), 1)
    rhs = (row_id == lane_id).astype(F32)
    wide = lambda v: jnp.broadcast_to(v[:1], (NZ, LANES))
    for s in (1, 2, 4, 8, 16, 32):
        back = lambda v: pltpu.roll(v, s, axis=1)
        forth = lambda v: pltpu.roll(v, LANES - s, axis=1)
        alpha = -low / back(mid)
        gamma = -up / forth(mid)
        rhs = rhs + wide(alpha) * back(rhs) + wide(gamma) * forth(rhs)
        mid = mid + alpha * back(up) + gamma * forth(low)
        low, up = alpha * back(low), gamma * forth(up)
    inverse = rhs / wide(mid)
    inverse = jnp.concatenate([inverse, jnp.zeros((LANES - NZ, LANES), F32)], axis=0)
    high = inverse.astype(BF16).astype(F32)
    weights = jnp.concatenate([high, inverse - high], axis=1)
    weights = jnp.concatenate([weights, weights], axis=0).astype(BF16)

    def solve(blocks):
        high, low = split(jnp.concatenate(blocks, axis=0))
        both = jnp.dot(jnp.concatenate([high, low], axis=1), weights, preferred_element_type=F32)
        return both[:, :LANES] + both[:, LANES:]

    row_id = lax.broadcasted_iota(jnp.int32, (ZS, LANES), 0)
    lane_id = lax.broadcasted_iota(jnp.int32, (ZS, LANES), 1)
    eye = ((row_id == lane_id) & (row_id < NZ)).astype(F32)
    profile = (lane_id >= 2) & (lane_id < NZ - 4)
    source = [((row_id == NZ + n) & profile).astype(F32) for n in range(STEPS + 1)]
    slope = jnp.broadcast_to(lat[:1], (ZS, LANES))

    degree = lambda p, n: 0 if n == 0 else n + p

    def get(p, n, k):
        if k > degree(p, n):
            return None
        return eye if n == 0 else poly_ref[p, n, k * ZS : (k + 1) * ZS, :]

    def total(*terms):
        terms = [(f, t) for f, t in terms if t is not None]
        result = None
        for f, t in terms:
            t = t if f in (1.0, -1.0) else f * t
            if result is None:
                result = -t if f == -1.0 else t
            else:
                result = result - t if f == -1.0 else result + t
        return result

    def step(p, n):
        count = degree(p, n + 1) + 1
        blocks, rest, last = [], [], None
        for k in range(count):
            u = get(p, n, k)
            if p == 0:
                kept, g, add = u, u, source[n]
            else:
                b, c = get(p - 1, n, k), get(p - 1, n + 1, k)
                if n == 0:
                    q = total((0.5, c), (-0.5, b))
                    add = 0.5 * source[0] + 0.5 * source[1]
                else:
                    q = total((7.0 / 12.0, c), (-8.0 / 12.0, b), (1.0 / 12.0, get(p - 1, n - 1, k)))
                    add = (-source[n - 1] + 8.0 * source[n] + 5.0 * source[n + 1]) * (1.0 / 12.0)
                kept = total((1.0, u), (-1.0, q))
                g = total((1.0, kept), (1.0, c), (-1.0, b))
                rest.append(q)
            spread = total((1.0, last), (-4.0, g))
            blocks.append(total((1.0, kept), (1.0, None if spread is None else slope * spread), (1.0, add if k == 0 else None)))
            last = g
        solved = solve(blocks)
        for k in range(count):
            block = solved[k * ZS : (k + 1) * ZS]
            if p > 0 and rest[k] is not None:
                block = block + rest[k]
            poly_ref[p, n + 1, k * ZS : (k + 1) * ZS, :] = block

    for p in range(LEVELS):
        first = (degree(p, STEPS) + 1) * ZS
        if first < POWERS * ZS:
            poly_ref[p, STEPS, first:, :] = jnp.zeros((POWERS * ZS - first, LANES), F32)
    for wave in range(STEPS + LEVELS - 1):
        for p in range(LEVELS):
            if 0 <= wave - p < STEPS:
                step(p, wave - p)

    level = place_ref[0]
    blank = jnp.zeros((SLOT - ZS, LANES), F32)
    for k in range(POWERS):
        block = poly_ref[level, STEPS, k * ZS : (k + 1) * ZS, :]
        block = jnp.concatenate([jnp.where(lane_id < NZ, block, 0.0), blank], axis=0)
        block = jnp.concatenate([block, pltpu.roll(block, SLOT, axis=1)], axis=0)
        high = block.astype(BF16).astype(F32)
        block = jnp.concatenate([high, block - high], axis=1).astype(BF16)
        out_ref[k, :LANES, :] = block
        out_ref[k, LANES:, :] = block


def advance(source, target, span, first, count, edge=lambda j, new: new):
    load = lambda i, j: source[first + i, 8 * j : 8 * j + 8, :]
    sublane = lax.broadcasted_iota(jnp.int32, (BLOCKS, LANES), 0)
    for start in range(0, span, CHUNK):
        inner = range(start, min(start + CHUNK, span))
        before = [load(-1, j) for j in inner]
        centre = [load(0, j) for j in inner]
        for i in range(count):
            after = [load(i + 1, j) for j in inner]
            if start == 0:
                low = jnp.where(sublane == 0, 0.0, pltpu.roll(load(i, span - 1), 1, axis=0))
            else:
                low = load(i, start - 1)
            if inner[-1] == span - 1:
                high = jnp.where(sublane == BLOCKS - 1, 0.0, pltpu.roll(load(i, 0), BLOCKS - 1, axis=0))
            else:
                high = load(i, inner[-1] + 1)
            line = [low] + centre + [high]
            for n, j in enumerate(inner):
                new = (before[n] + after[n]) + (line[n] + line[n + 2])
                target[first + i, 8 * j : 8 * j + 8, :] = edge(j, new)
            before, centre = centre, after


def powers(fields, total_ref, coef_ref, span, edge, above, below):
    for k in range(POWERS):
        source, target = fields[k % 2], fields[1 - k % 2]
        cells = source[HALO : HALO + HALF].reshape(HALF * span * BLOCKS, LANES)
        high, low = split(cells)
        both = jnp.dot(jnp.concatenate([high, low], axis=1), coef_ref[k], preferred_element_type=F32)
        both = (both[:, :LANES] + both[:, LANES:]).reshape(HALF, span * BLOCKS, LANES)
        total_ref[...] = both if k == 0 else total_ref[...] + both
        if k + 1 < POWERS:
            advance(source, target, span, HALO, HALF, edge)
        if k + 1 < HALO:
            count = HALO - k - 1
            advance(source, target, span, k + 1, count, lambda j, new: edge(j, new) * above)
            advance(source, target, span, HALO + HALF, count, lambda j, new: edge(j, new) * below)


def grid_rows(place_ref):
    lane = lax.broadcasted_iota(jnp.int32, (BLOCKS, LANES), 1)
    above = jnp.where((lane < SLOT) & (place_ref[1] == 0), 0.0, 1.0)
    below = jnp.where((lane >= SLOT) & (place_ref[1] == place_ref[3]), 0.0, 1.0)
    return above, below


def bulk(
    place_ref, rates_ref, plan_ref, x_ref, y_ref, cells_ref, u_ref, far_ref, near_ref,
    early_centre_ref, early_left_ref, early_right_ref, coef_ref, out_ref, left_ref, right_ref,
    line_ref, field_ref, other_field_ref, total_ref, src_ref,
):
    late = is_late(place_ref)

    @pl.when(late)
    def _():
        sources(place_ref, rates_ref, plan_ref, x_ref, y_ref, cells_ref, src_ref, left_ref, right_ref)

    @pl.when(jnp.logical_not(late))
    def _():
        src_ref[...] = early_centre_ref[...]
        left_ref[...] = early_left_ref[...]
        right_ref[...] = early_right_ref[...]

    ty = place_ref[2]
    even = lax.rem(place_ref[1], 2) == 0
    sublane = lax.broadcasted_iota(jnp.int32, (BLOCKS, LANES), 0)
    blank = jnp.zeros((SLOT - ZS, LANES), F32)
    room = jnp.zeros((BACK, LANES), F32)
    for i in range(PAIRS):
        rows = []
        for r in (i, i + HALF):
            rows += [ext_row(r, even, u_ref, far_ref, near_ref), src_ref[8 * r : 8 * r + 8, :], blank]
        line_ref[i, :BACK, :] = room
        line_ref[i, BACK : BACK + LANES, :] = jnp.concatenate(rows, axis=0).T
        line_ref[i, BACK + LANES :, :] = room
        for j in range(SPAN):
            field_ref[i, 8 * j : 8 * j + 8, :] = line_ref[i, pl.ds(j, BLOCKS, stride=SPAN), :]
    left = jnp.where((sublane == 0) & (ty == 0), 0.0, 1.0)
    right = jnp.where((sublane == BLOCKS - 1) & (ty == place_ref[4]), 0.0, 1.0)

    def edge(j, new):
        return new * left if j < BACK else new * right if j >= SPAN - BACK else new

    powers((field_ref, other_field_ref), total_ref, coef_ref, SPAN, edge, *grid_rows(place_ref))
    for i in range(HALF):
        for j in range(SPAN):
            line_ref[i, pl.ds(j, BLOCKS, stride=SPAN), :] = total_ref[i, 8 * j : 8 * j + 8, :]
        out_ref[i] = line_ref[i, BACK : BACK + LANES, :]


def rim(
    place_ref, own_ref, other_ref, src_left_ref, src_right_ref, coef_ref, bulk_ref,
    out_ref, line_ref, side_ref, field_ref, other_field_ref, total_ref, result_ref, sems,
):
    low_level = place_ref[0] < 2
    blank = jnp.zeros((SLOT - ZS, LANES), F32)
    for side, src_ref in enumerate((src_left_ref, src_right_ref)):
        for t in range(TILES):
            part = slice(t * LANES, (t + 1) * LANES)
            tile = jnp.where(low_level == (side == 0), own_ref[t], other_ref[t])
            side_ref[side, part, :] = jnp.concatenate([tile, src_ref[:, part], blank] * 2, axis=0).T

    def halo_of(side, r):
        t, first, width = PIECES.get(r, (0, 0, HALO))
        first = t * LANES + first + (width - HALO if side == 0 else 0)
        return side_ref[side, first : first + HALO, :]

    in_low_half = lax.broadcasted_iota(jnp.int32, (HALO, LANES), 1) < SLOT
    room = jnp.zeros((2 * (RIM - HALO), LANES), F32)
    for i in range(PAIRS):
        line_ref[i, :HALO, :] = jnp.where(in_low_half, halo_of(0, i), halo_of(0, i + HALF))
        line_ref[i, HALO : 2 * RIM - HALO, :] = room
        line_ref[i, 2 * RIM - HALO :, :] = jnp.where(in_low_half, halo_of(1, i), halo_of(1, i + HALF))
        for j in range(RIM_SPAN):
            field_ref[i, 8 * j : 8 * j + 8, :] = line_ref[i, pl.ds(j, BLOCKS, stride=RIM_SPAN), :]
    powers((field_ref, other_field_ref), total_ref, coef_ref, RIM_SPAN, lambda j, new: new, *grid_rows(place_ref))
    copies = []
    for i in range(HALF):
        for j in range(RIM_SPAN):
            line_ref[i, pl.ds(j, BLOCKS, stride=RIM_SPAN), :] = total_ref[i, 8 * j : 8 * j + 8, :]
        inner = LANES - 2 * (RIM - HALO)
        change = [line_ref[i, HALO:RIM, :], jnp.zeros((inner, LANES), F32), line_ref[i, RIM : 2 * RIM - HALO, :]]
        result = (bulk_ref[i] + jnp.concatenate(change, axis=0)).T
        group, row = divmod(i, 8)
        result_ref[group, pl.ds(row, NZ, stride=8), :] = result[:NZ]
        result_ref[group + 2, pl.ds(row, NZ, stride=8), :] = result[SLOT : SLOT + NZ]
        if row == 7:
            for g in (group, group + 2):
                copies.append(pltpu.make_async_copy(result_ref.at[g].reshape(NZ, 8, LANES), out_ref.at[:, pl.ds(8 * g, 8), :], sems.at[g]))
                copies[-1].start()
    for copy in copies:
        copy.wait()


SMEM = pl.BlockSpec(memory_space=pltpu.SMEM)
WHOLE = pl.BlockSpec(memory_space=pltpu.VMEM)


def call(kernel, name, ins, outs, scratch=(), cost=0, out_spec=None):
    return pl.pallas_call(
        kernel,
        out_shape=outs,
        in_specs=ins,
        out_specs=out_spec or jax.tree.map(lambda _: WHOLE, outs),
        scratch_shapes=list(scratch),
        compiler_params=pltpu.CompilerParams(vmem_limit_bytes=VMEM),
        cost_estimate=pl.CostEstimate(flops=cost, bytes_accessed=1 << 20, transcendentals=0),
        name=name,
    )


def on_device(initial, layer_ids, lateral_number, vertical_number, pulse_rates, bore_x, bore_y, plan):
    shape = lambda *s, dtype=F32: jax.ShapeDtypeStruct(s, dtype)
    count_x, count_y = lax.axis_size("tx"), lax.axis_size("ty")
    indices = [lax.axis_index(name) for name in ("level", "tx", "ty")]
    place = jnp.stack(indices + [jnp.int32(count_x - 1), jnp.int32(count_y - 1)])
    flat = initial.reshape(NZ * ROWS, LANES)
    slab = shape(HALO, NZ, LANES)
    whole = shape(NZ * ROWS, LANES)
    far, near, kept = call(edge_rows, "edge_rows", [SMEM, WHOLE], (slab, slab, whole), cost=800 << 20)(place, flat)
    pairs = lambda first: [(i + a, i + 1 - a) for i in range(first, count_x - 1, 2) for a in (0, 1)]
    far = lax.ppermute(far, "tx", pairs(1))
    near = lax.ppermute(near, "tx", pairs(0))
    packed = shape(TILES, NZ, LANES)
    strips = call(own_columns, "own_columns", [SMEM, WHOLE], packed, cost=1000 << 20)(place, kept)
    sides = shape(8, TILES * LANES)
    planes = (shape(ZS * 8, LANES), sides, sides)
    bores = (pulse_rates, plan.T, bore_x[None, :], bore_y[None, :], side_cells())
    src = call(early_sources, "early_sources", [SMEM] * 2 + [WHOLE] * 4, planes, cost=1700 << 20)(place, *bores)
    strips, src = lax.optimization_barrier((strips, src))
    strips = call(edge_columns, "edge_columns", [SMEM] + [WHOLE] * 3, packed, cost=800 << 20)(
        place, strips, far, near
    )
    ids = jnp.pad(layer_ids, (0, LANES - NZ))[None, :]
    strips, ids = lax.optimization_barrier((strips, ids))
    route = []
    for i in range(count_y - 1):
        for l in (0, 1):
            route.append(((l + 2) * count_y + i, l * count_y + i + 1))
            route.append((l * count_y + i + 1, (l + 2) * count_y + i))
    own = lax.ppermute(strips, ("level", "ty"), route)
    table = call(
        coefs,
        "coefs",
        [SMEM] * 3 + [WHOLE],
        shape(POWERS, 2 * LANES, 2 * LANES, dtype=BF16),
        [pltpu.VMEM((LEVELS, STEPS + 1, POWERS * ZS, LANES), F32)],
        cost=4600 << 20,
    )(place, lateral_number, vertical_number, ids)
    own, table = lax.optimization_barrier((own, table))
    other = lax.ppermute(own, "level", [(0, 2), (2, 0), (1, 3), (3, 1)])
    room = lambda span: [pltpu.VMEM((PAIRS, span * BLOCKS, LANES), F32)]
    total = lambda span: [pltpu.VMEM((HALF, span * BLOCKS, LANES), F32)]
    inner, src_left, src_right = call(
        bulk,
        "bulk",
        [SMEM] * 2 + [WHOLE] * 11,
        (shape(HALF, LANES, LANES), sides, sides),
        room(SPAN) * 3 + total(SPAN) + [pltpu.VMEM((ZS * 8, LANES), F32)],
        cost=8000 << 20,
    )(place, *bores, kept, far, near, *src, table)
    result = call(
        rim,
        "rim",
        [SMEM] + [WHOLE] * 6,
        shape(NZ, ROWS, LANES),
        room(RIM_SPAN)
        + [pltpu.VMEM((2, TILES * LANES, LANES), F32)]
        + room(RIM_SPAN) * 2
        + total(RIM_SPAN)
        + [pltpu.VMEM((ROWS // 8, NZ * 8, LANES), F32), pltpu.SemaphoreType.DMA((ROWS // 8,))],
        out_spec=pl.BlockSpec(memory_space=pl.ANY),
        cost=4000 << 20,
    )(place, own, other, src_left, src_right, table, inner)
    return result.reshape(1, NZ, ROWS, LANES)


def solution(mesh):
    return jax.shard_map(
        on_device,
        mesh=mesh,
        in_specs=(P(None, "tx", "ty"), P(), P(), P(), P(), P(), P(), P()),
        out_specs=P("level", None, "tx", "ty"),
        check_vma=False,
    )
```

```python
import jax
import jax.numpy as jnp
import numpy as np
from jax import lax
from jax.experimental import pallas as pl
from jax.experimental.pallas import tpu as pltpu
from jax.sharding import PartitionSpec as P

NZ = 48
STEPS = 6
NLAYER = 6
NPULSE = 8
LEVELS = 4
POWERS = STEPS + LEVELS
HALO = POWERS - 1
ROWS = 32
LANES = 128
EXT = ROWS + 2 * HALO
ZS = NZ + 8
HALF = ROWS // 2
PAIRS = HALF + 2 * HALO
SLOT = LANES // 2
LINE = 4
BLOCKS = 8
BACK = (POWERS - 1) // 2
SPAN = (LANES + 2 * BACK) // BLOCKS
RIM = 20
RIM_SPAN = 2 * RIM // BLOCKS
CHUNK = 5
VMEM = 48 * 1024 * 1024
F32, BF16 = jnp.float32, jnp.bfloat16


def pieces():
    width = [HALO - max(HALO - r, r - (HALO + ROWS - 1), 0) for r in range(EXT)]
    slots = [[r] for r in range(EXT) if width[r] == HALO]
    for d in range(1, (HALO + 1) // 2):
        slots.append([HALO - d, d])
        slots.append([EXT - 1 - (HALO - d), EXT - 1 - d])
    where, per_tile = {}, LANES // HALO
    for n, rows in enumerate(slots):
        lane = HALO * (n % per_tile)
        for r in rows:
            where[r] = (n // per_tile, lane, width[r])
            lane += width[r]
    return where, -(-len(slots) // per_tile)


PIECES, TILES = pieces()


def split(x):
    high = x.astype(BF16)
    return high, (x - high.astype(F32)).astype(BF16)


def edge_rows(place, u_ref, far_ref, near_ref, kept_ref):
    even = lax.rem(place[1], 2) == 0
    for i in range(HALO):
        first = u_ref[pl.ds(i, NZ, stride=ROWS), :]
        last = u_ref[pl.ds(ROWS - HALO + i, NZ, stride=ROWS), :]
        far_ref[i] = jnp.where(even, first, last)
        near_ref[i] = jnp.where(even, last, first)
    kept_ref[...] = u_ref[...]


def ext_row(r, even, u_ref, far_ref, near_ref):
    if r < HALO:
        return jnp.where(even, far_ref[r], near_ref[r])
    if r < HALO + ROWS:
        return u_ref[pl.ds(r - HALO, NZ, stride=ROWS), :]
    return jnp.where(even, near_ref[r - HALO - ROWS], far_ref[r - HALO - ROWS])


def pack(place, rows, row_of, packed_ref, tiles):
    lane = lax.broadcasted_iota(jnp.int32, (NZ, LANES), 1)
    send_last = place[0] >= 2
    for r in rows:
        t, first, width = PIECES[r]
        row = pltpu.roll(row_of(r), first + jnp.where(send_last, width, 0), axis=1)
        tiles[t] = jnp.where((lane >= first) & (lane < first + width), row, tiles[t])
    for t in range(TILES):
        packed_ref[t] = tiles[t]


def own_columns(place, u_ref, packed_ref):
    row_of = lambda r: u_ref[pl.ds(r - HALO, NZ, stride=ROWS), :]
    pack(place, range(HALO, HALO + ROWS), row_of, packed_ref, [jnp.zeros((NZ, LANES), F32)] * TILES)


def edge_columns(place, strips_ref, far_ref, near_ref, packed_ref):
    even = lax.rem(place[1], 2) == 0
    rows = [r for r in PIECES if not HALO <= r < HALO + ROWS]
    row_of = lambda r: ext_row(r, even, None, far_ref, near_ref)
    pack(place, rows, row_of, packed_ref, [strips_ref[t] for t in range(TILES)])


def side_cells():
    cells = np.full((8, TILES * LANES), -(1 << 20), np.float32)
    for r, (t, first, width) in PIECES.items():
        for c in range(width):
            cells[:3, t * LANES + first + c] = (r - HALO, c - width, LANES + c)
    return cells


def is_late(place):
    return lax.rem(place[2], LINE) == LINE - 1


def early_sources(place, *refs):
    pl.when(jnp.logical_not(is_late(place)))(lambda: sources(place, *refs))


def sources(place, rates_ref, plan_ref, x_ref, y_ref, cells_ref, centre_ref, left_ref, right_ref):
    bores = plan_ref.shape[1]
    plan = plan_ref[...]
    rate = jnp.zeros(plan.shape, F32)
    for j in range(NPULSE):
        rate = jnp.where(plan == j, rates_ref[:, j : j + 1], rate)
    rate = jnp.concatenate([rate, jnp.zeros((1, bores), F32)], axis=0)
    rate_high = rate.astype(BF16).astype(F32)
    rate_low = rate - rate_high
    x = x_ref[...] - place[1] * ROWS
    y = y_ref[...] - place[2] * LANES
    hit_x = x == lax.broadcasted_iota(jnp.int32, (ZS, bores), 0) - HALO
    hit_y = (y == lax.broadcasted_iota(jnp.int32, (LANES, bores), 0)).astype(F32).astype(BF16)
    contract = lambda p, q: lax.dot_general(p, q, (((1,), (1,)), ((), ())), preferred_element_type=F32)

    def plane(rates):
        left = [jnp.where(hit_x, rates[m : m + 1], 0.0) for m in range(STEPS + 1)]
        return contract(jnp.concatenate(left, axis=0).astype(BF16), hit_y)

    both = plane(rate_high) + plane(rate_low)
    for m in range(STEPS + 1):
        centre_ref[pl.ds(m, ZS, stride=8), :] = both[m * ZS : (m + 1) * ZS]
    centre_ref[pl.ds(7, ZS, stride=8), :] = jnp.zeros((ZS, LANES), F32)
    rates = jnp.concatenate([rate_high, rate_low], axis=0).astype(BF16)
    columns = [cells_ref[:, t * LANES : (t + 1) * LANES].T for t in range(TILES)]
    columns = jnp.concatenate(columns, axis=0).astype(jnp.int32)
    for side, ref in ((1, left_ref), (2, right_ref)):
        hit = (x == columns[:, :1]) & (y == columns[:, side : side + 1])
        both = contract(rates, hit.astype(F32).astype(BF16))
        ref[...] = both[:8] + both[8:]


def coefs(place, lateral_ref, vertical_ref, ids_ref, out_ref, poly_ref):
    ids = jnp.broadcast_to(ids_ref[...], (8, LANES))
    lane = lax.broadcasted_iota(jnp.int32, (8, LANES), 1)
    cond, lat = jnp.zeros((8, LANES), F32), jnp.zeros((8, LANES), F32)
    for j in range(NLAYER):
        cond = jnp.where(ids == j, vertical_ref[:, j : j + 1], cond)
        lat = jnp.where(ids == j, lateral_ref[:, j : j + 1], lat)
    cond = jnp.where(lane < NZ, cond, 1.0)
    lat = jnp.where(lane < NZ, lat, 0.0)
    after = pltpu.roll(cond, LANES - 1, axis=1)
    link = jnp.where(lane < NZ - 1, 2.0 * cond * after / (cond + after), 0.0)
    before = pltpu.roll(link, 1, axis=1)
    low, up = -before, -link
    mid = 1.0 + (jnp.where(lane == 0, cond, 0.0) + link + before)
    mid = jnp.where(lane < NZ, mid, 1.0)
    row_id = lax.broadcasted_iota(jnp.int32, (NZ, LANES), 0)
    lane_id = lax.broadcasted_iota(jnp.int32, (NZ, LANES), 1)
    rhs = (row_id == lane_id).astype(F32)
    wide = lambda v: jnp.broadcast_to(v[:1], (NZ, LANES))
    for s in (1, 2, 4, 8, 16, 32):
        back = lambda v: pltpu.roll(v, s, axis=1)
        forth = lambda v: pltpu.roll(v, LANES - s, axis=1)
        alpha = -low / back(mid)
        gamma = -up / forth(mid)
        rhs = rhs + wide(alpha) * back(rhs) + wide(gamma) * forth(rhs)
        mid = mid + alpha * back(up) + gamma * forth(low)
        low, up = alpha * back(low), gamma * forth(up)
    inverse = rhs / wide(mid)
    inverse = jnp.concatenate([inverse, jnp.zeros((LANES - NZ, LANES), F32)], axis=0)
    high = inverse.astype(BF16).astype(F32)
    weights = jnp.concatenate([high, inverse - high], axis=1)
    weights = jnp.concatenate([weights, weights], axis=0).astype(BF16)

    def solve(blocks):
        high, low = split(jnp.concatenate(blocks, axis=0))
        both = jnp.dot(jnp.concatenate([high, low], axis=1), weights, preferred_element_type=F32)
        return both[:, :LANES] + both[:, LANES:]

    row_id = lax.broadcasted_iota(jnp.int32, (ZS, LANES), 0)
    lane_id = lax.broadcasted_iota(jnp.int32, (ZS, LANES), 1)
    eye = ((row_id == lane_id) & (row_id < NZ)).astype(F32)
    profile = (lane_id >= 2) & (lane_id < NZ - 4)
    source = [((row_id == NZ + n) & profile).astype(F32) for n in range(STEPS + 1)]
    slope = jnp.broadcast_to(lat[:1], (ZS, LANES))

    degree = lambda p, n: 0 if n == 0 else n + p

    def get(p, n, k):
        if k > degree(p, n):
            return None
        return eye if n == 0 else poly_ref[p, n, k * ZS : (k + 1) * ZS, :]

    def total(*terms):
        terms = [(f, t) for f, t in terms if t is not None]
        result = None
        for f, t in terms:
            t = t if f in (1.0, -1.0) else f * t
            if result is None:
                result = -t if f == -1.0 else t
            else:
                result = result - t if f == -1.0 else result + t
        return result

    def step(p, n):
        count = degree(p, n + 1) + 1
        blocks, rest, last = [], [], None
        for k in range(count):
            u = get(p, n, k)
            if p == 0:
                kept, g, add = u, u, source[n]
            else:
                b, c = get(p - 1, n, k), get(p - 1, n + 1, k)
                if n == 0:
                    q = total((0.5, c), (-0.5, b))
                    add = 0.5 * source[0] + 0.5 * source[1]
                else:
                    q = total((7.0 / 12.0, c), (-8.0 / 12.0, b), (1.0 / 12.0, get(p - 1, n - 1, k)))
                    add = (-source[n - 1] + 8.0 * source[n] + 5.0 * source[n + 1]) * (1.0 / 12.0)
                kept = total((1.0, u), (-1.0, q))
                g = total((1.0, kept), (1.0, c), (-1.0, b))
                rest.append(q)
            spread = total((1.0, last), (-4.0, g))
            blocks.append(total((1.0, kept), (1.0, None if spread is None else slope * spread), (1.0, add if k == 0 else None)))
            last = g
        solved = solve(blocks)
        for k in range(count):
            block = solved[k * ZS : (k + 1) * ZS]
            if p > 0 and rest[k] is not None:
                block = block + rest[k]
            poly_ref[p, n + 1, k * ZS : (k + 1) * ZS, :] = block

    for p in range(LEVELS):
        first = (degree(p, STEPS) + 1) * ZS
        if first < POWERS * ZS:
            poly_ref[p, STEPS, first:, :] = jnp.zeros((POWERS * ZS - first, LANES), F32)
    for wave in range(STEPS + LEVELS - 1):
        for p in range(LEVELS):
            if 0 <= wave - p < STEPS:
                step(p, wave - p)

    level = place[0]
    blank = jnp.zeros((SLOT - ZS, LANES), F32)
    for k in range(POWERS):
        block = poly_ref[level, STEPS, k * ZS : (k + 1) * ZS, :]
        block = jnp.concatenate([jnp.where(lane_id < NZ, block, 0.0), blank], axis=0)
        block = jnp.concatenate([block, pltpu.roll(block, SLOT, axis=1)], axis=0)
        high = block.astype(BF16).astype(F32)
        block = jnp.concatenate([high, block - high], axis=1).astype(BF16)
        out_ref[k, :LANES, :] = block
        out_ref[k, LANES:, :] = block


def advance(source, target, span, first, count, edge=lambda j, new: new):
    load = lambda i, j: source[first + i, 8 * j : 8 * j + 8, :]
    sublane = lax.broadcasted_iota(jnp.int32, (BLOCKS, LANES), 0)
    for start in range(0, span, CHUNK):
        inner = range(start, min(start + CHUNK, span))
        before = [load(-1, j) for j in inner]
        centre = [load(0, j) for j in inner]
        for i in range(count):
            after = [load(i + 1, j) for j in inner]
            if start == 0:
                low = jnp.where(sublane == 0, 0.0, pltpu.roll(load(i, span - 1), 1, axis=0))
            else:
                low = load(i, start - 1)
            if inner[-1] == span - 1:
                high = jnp.where(sublane == BLOCKS - 1, 0.0, pltpu.roll(load(i, 0), BLOCKS - 1, axis=0))
            else:
                high = load(i, inner[-1] + 1)
            line = [low] + centre + [high]
            for n, j in enumerate(inner):
                new = (before[n] + after[n]) + (line[n] + line[n + 2])
                target[first + i, 8 * j : 8 * j + 8, :] = edge(j, new)
            before, centre = centre, after


def powers(fields, total_ref, coef_ref, span, edge, above, below):
    for k in range(POWERS):
        source, target = fields[k % 2], fields[1 - k % 2]
        cells = source[HALO : HALO + HALF].reshape(HALF * span * BLOCKS, LANES)
        high, low = split(cells)
        both = jnp.dot(jnp.concatenate([high, low], axis=1), coef_ref[k], preferred_element_type=F32)
        both = (both[:, :LANES] + both[:, LANES:]).reshape(HALF, span * BLOCKS, LANES)
        total_ref[...] = both if k == 0 else total_ref[...] + both
        if k + 1 < POWERS:
            advance(source, target, span, HALO, HALF, edge)
        if k + 1 < HALO:
            count = HALO - k - 1
            advance(source, target, span, k + 1, count, lambda j, new: edge(j, new) * above)
            advance(source, target, span, HALO + HALF, count, lambda j, new: edge(j, new) * below)


def grid_rows(place):
    lane = lax.broadcasted_iota(jnp.int32, (BLOCKS, LANES), 1)
    above = jnp.where((lane < SLOT) & (place[1] == 0), 0.0, 1.0)
    below = jnp.where((lane >= SLOT) & (place[1] == place[3]), 0.0, 1.0)
    return above, below


def bulk(
    place, rates_ref, plan_ref, x_ref, y_ref, cells_ref, u_ref, far_ref, near_ref,
    early_centre_ref, early_left_ref, early_right_ref, coef_ref, out_ref, left_ref, right_ref,
    line_ref, field_ref, other_field_ref, total_ref, src_ref,
):
    late = is_late(place)

    @pl.when(late)
    def _():
        sources(place, rates_ref, plan_ref, x_ref, y_ref, cells_ref, src_ref, left_ref, right_ref)

    @pl.when(jnp.logical_not(late))
    def _():
        src_ref[...] = early_centre_ref[...]
        left_ref[...] = early_left_ref[...]
        right_ref[...] = early_right_ref[...]

    ty = place[2]
    even = lax.rem(place[1], 2) == 0
    sublane = lax.broadcasted_iota(jnp.int32, (BLOCKS, LANES), 0)
    blank = jnp.zeros((SLOT - ZS, LANES), F32)
    room = jnp.zeros((BACK, LANES), F32)
    for i in range(PAIRS):
        rows = []
        for r in (i, i + HALF):
            rows += [ext_row(r, even, u_ref, far_ref, near_ref), src_ref[8 * r : 8 * r + 8, :], blank]
        line_ref[i, :BACK, :] = room
        line_ref[i, BACK : BACK + LANES, :] = jnp.concatenate(rows, axis=0).T
        line_ref[i, BACK + LANES :, :] = room
        for j in range(SPAN):
            field_ref[i, 8 * j : 8 * j + 8, :] = line_ref[i, pl.ds(j, BLOCKS, stride=SPAN), :]
    left = jnp.where((sublane == 0) & (ty == 0), 0.0, 1.0)
    right = jnp.where((sublane == BLOCKS - 1) & (ty == place[4]), 0.0, 1.0)

    def edge(j, new):
        return new * left if j < BACK else new * right if j >= SPAN - BACK else new

    powers((field_ref, other_field_ref), total_ref, coef_ref, SPAN, edge, *grid_rows(place))
    for i in range(HALF):
        for j in range(SPAN):
            line_ref[i, pl.ds(j, BLOCKS, stride=SPAN), :] = total_ref[i, 8 * j : 8 * j + 8, :]
        out_ref[i] = line_ref[i, BACK : BACK + LANES, :]


def rim(
    place, own_ref, other_ref, src_left_ref, src_right_ref, coef_ref, bulk_ref,
    out_ref, line_ref, side_ref, field_ref, other_field_ref, total_ref, result_ref, sems,
):
    low_level = place[0] < 2
    blank = jnp.zeros((SLOT - ZS, LANES), F32)
    for side, src_ref in enumerate((src_left_ref, src_right_ref)):
        for t in range(TILES):
            part = slice(t * LANES, (t + 1) * LANES)
            tile = jnp.where(low_level == (side == 0), own_ref[t], other_ref[t])
            side_ref[side, part, :] = jnp.concatenate([tile, src_ref[:, part], blank] * 2, axis=0).T

    def halo_of(side, r):
        t, first, width = PIECES.get(r, (0, 0, HALO))
        first = t * LANES + first + (width - HALO if side == 0 else 0)
        return side_ref[side, first : first + HALO, :]

    in_low_half = lax.broadcasted_iota(jnp.int32, (HALO, LANES), 1) < SLOT
    room = jnp.zeros((2 * (RIM - HALO), LANES), F32)
    for i in range(PAIRS):
        line_ref[i, :HALO, :] = jnp.where(in_low_half, halo_of(0, i), halo_of(0, i + HALF))
        line_ref[i, HALO : 2 * RIM - HALO, :] = room
        line_ref[i, 2 * RIM - HALO :, :] = jnp.where(in_low_half, halo_of(1, i), halo_of(1, i + HALF))
        for j in range(RIM_SPAN):
            field_ref[i, 8 * j : 8 * j + 8, :] = line_ref[i, pl.ds(j, BLOCKS, stride=RIM_SPAN), :]
    powers((field_ref, other_field_ref), total_ref, coef_ref, RIM_SPAN, lambda j, new: new, *grid_rows(place))
    copies = []
    for i in range(HALF):
        for j in range(RIM_SPAN):
            line_ref[i, pl.ds(j, BLOCKS, stride=RIM_SPAN), :] = total_ref[i, 8 * j : 8 * j + 8, :]
        inner = LANES - 2 * (RIM - HALO)
        change = [line_ref[i, HALO:RIM, :], jnp.zeros((inner, LANES), F32), line_ref[i, RIM : 2 * RIM - HALO, :]]
        result = (bulk_ref[i] + jnp.concatenate(change, axis=0)).T
        group, row = divmod(i, 8)
        result_ref[group, pl.ds(row, NZ, stride=8), :] = result[:NZ]
        result_ref[group + 2, pl.ds(row, NZ, stride=8), :] = result[SLOT : SLOT + NZ]
        if row == 7:
            for g in (group, group + 2):
                copies.append(pltpu.make_async_copy(result_ref.at[g].reshape(NZ, 8, LANES), out_ref.at[:, pl.ds(8 * g, 8), :], sems.at[g]))
                copies[-1].start()
    for copy in copies:
        copy.wait()


WHOLE = pl.BlockSpec(memory_space=pltpu.VMEM)


def call(kernel, name, ins, outs, scratch=(), cost=0, out_spec=None):
    def with_place(*refs):
        sizes = [lax.axis_size(name) for name in ("tx", "ty")]
        kernel([lax.axis_index(name) for name in ("level", "tx", "ty")] + [size - 1 for size in sizes], *refs)

    return pl.pallas_call(
        with_place,
        out_shape=outs,
        in_specs=ins,
        out_specs=out_spec or jax.tree.map(lambda _: WHOLE, outs),
        scratch_shapes=list(scratch),
        compiler_params=pltpu.CompilerParams(vmem_limit_bytes=VMEM),
        cost_estimate=pl.CostEstimate(flops=cost, bytes_accessed=1 << 20, transcendentals=0),
        name=name,
    )


def on_device(initial, layer_ids, lateral_number, vertical_number, pulse_rates, bore_x, bore_y, plan):
    shape = lambda *s, dtype=F32: jax.ShapeDtypeStruct(s, dtype)
    count_x, count_y = lax.axis_size("tx"), lax.axis_size("ty")
    flat = initial.reshape(NZ * ROWS, LANES)
    slab = shape(HALO, NZ, LANES)
    whole = shape(NZ * ROWS, LANES)
    far, near, kept = call(edge_rows, "edge_rows", [WHOLE], (slab, slab, whole), cost=800 << 20)(flat)
    pairs = lambda first: [(i + a, i + 1 - a) for i in range(first, count_x - 1, 2) for a in (0, 1)]
    far = lax.ppermute(far, "tx", pairs(1))
    near = lax.ppermute(near, "tx", pairs(0))
    packed = shape(TILES, NZ, LANES)
    strips = call(own_columns, "own_columns", [WHOLE], packed, cost=1000 << 20)(kept)
    sides = shape(8, TILES * LANES)
    planes = (shape(ZS * 8, LANES), sides, sides)
    bores = (pulse_rates[None, :], plan.T, bore_x[None, :], bore_y[None, :], side_cells())
    src = call(early_sources, "early_sources", [WHOLE] * 5, planes, cost=1700 << 20)(*bores)
    strips, src = lax.optimization_barrier((strips, src))
    strips = call(edge_columns, "edge_columns", [WHOLE] * 3, packed, cost=800 << 20)(strips, far, near)
    ids = jnp.pad(layer_ids, (0, LANES - NZ))[None, :]
    strips, ids = lax.optimization_barrier((strips, ids))
    route = []
    for i in range(count_y - 1):
        for l in (0, 1):
            route.append(((l + 2) * count_y + i, l * count_y + i + 1))
            route.append((l * count_y + i + 1, (l + 2) * count_y + i))
    own = lax.ppermute(strips, ("level", "ty"), route)
    table = call(
        coefs,
        "coefs",
        [WHOLE] * 3,
        shape(POWERS, 2 * LANES, 2 * LANES, dtype=BF16),
        [pltpu.VMEM((LEVELS, STEPS + 1, POWERS * ZS, LANES), F32)],
        cost=4600 << 20,
    )(lateral_number[None, :], vertical_number[None, :], ids)
    own, table = lax.optimization_barrier((own, table))
    other = lax.ppermute(own, "level", [(0, 2), (2, 0), (1, 3), (3, 1)])
    room = lambda span: [pltpu.VMEM((PAIRS, span * BLOCKS, LANES), F32)]
    total = lambda span: [pltpu.VMEM((HALF, span * BLOCKS, LANES), F32)]
    inner, src_left, src_right = call(
        bulk,
        "bulk",
        [WHOLE] * 12,
        (shape(HALF, LANES, LANES), sides, sides),
        room(SPAN) * 3 + total(SPAN) + [pltpu.VMEM((ZS * 8, LANES), F32)],
        cost=8000 << 20,
    )(*bores, kept, far, near, *src, table)
    result = call(
        rim,
        "rim",
        [WHOLE] * 6,
        shape(NZ, ROWS, LANES),
        room(RIM_SPAN)
        + [pltpu.VMEM((2, TILES * LANES, LANES), F32)]
        + room(RIM_SPAN) * 2
        + total(RIM_SPAN)
        + [pltpu.VMEM((ROWS // 8, NZ * 8, LANES), F32), pltpu.SemaphoreType.DMA((ROWS // 8,))],
        out_spec=pl.BlockSpec(memory_space=pl.ANY),
        cost=4000 << 20,
    )(own, other, src_left, src_right, table, inner)
    return result.reshape(1, NZ, ROWS, LANES)


def solution(mesh):
    return jax.shard_map(
        on_device,
        mesh=mesh,
        in_specs=(P(None, "tx", "ty"), P(), P(), P(), P(), P(), P(), P()),
        out_specs=P("level", None, "tx", "ty"),
        check_vma=False,
    )
```
